256 devices in a mesh: seq: 64 (over y_lo, x, z), batch: 4 (over y_hi, core).
Axes of the slice: x: 4, y: 4 (y_hi: 2, y_lo: 2; y = y_hi * 2 + y_lo), z: 8, core: 2. Of those that a mesh axis runs over, the one named last changes fastest.
Arguments:
- queries: bfloat16 [512, 1024], replicated, may hold values from -48 to 48
- inputs: bfloat16 [4, 49152, 1024], P('batch', 'seq'), may hold values from -18 to 18
- cotangent: bfloat16 [4, 512, 1024], P('batch'), may hold values from -48 to 48
- key_weight: bfloat16 [1024, 1024], replicated, may hold values from -0.1875 to 0.1875
- value_weight: bfloat16 [1024, 1024], replicated, may hold values from -0.1875 to 0.1875
Outputs:
- input_grad: bfloat16 [4, 49152, 1024], P('batch', 'seq')
- latent_grad: float32 [512, 1024], P('seq')
- key_weight_grad: float32 [1024, 1024], P('seq')
- value_weight_grad: float32 [1024, 1024], P('seq')
The draws below stay inside these ranges and needn't reach their ends.
All inputs are finite; a program needn't handle non-finite values.
Results may differ from the reference program's by a relative error of at most 0.015.
The reference program's roundings to bfloat16 on the way count: a program that leaves them out, or rounds other values in their place, can miss the bound.
Values sent between devices are 32-bit elements; how exact they have to be, the bound alone decides.
No kernel may reach another device: no remote copies, remote signals or barrier semaphores. Data moves between devices by JAX's collectives and lax.ppermute only.
A program may use at most 128 MiB of HBM per device.

```python
import jax
import jax.numpy as jnp
from jax import lax

L = 512
D = 1024
H = 8
HS = 128
C = 1024
M = 49152
EXAMPLES = 4


def draw_queries(key, part):
    key = jax.random.fold_in(key, 11)
    base_key = jax.random.fold_in(key, 0)
    values = jnp.clip(jax.random.normal(base_key, (L, D), jnp.float32), -6.0, 6.0)
    return values.astype(jnp.bfloat16)


def draw_inputs(key, part):
    key = jax.random.fold_in(key, 23)
    base_key = jax.random.fold_in(key, 0)
    ramp = jnp.sqrt(1.0 + 2.5 * jnp.arange(M, dtype=jnp.float32) / M)
    values = jnp.clip(jax.random.normal(base_key, (EXAMPLES, M, C), jnp.float32), -6.0, 6.0)
    return (values * ramp[None, :, None]).astype(jnp.bfloat16)


def levels(stream_key, dims, cuts, smallest, largest):
    loudness = 1.0
    for position, blocks in cuts:
        draws = jax.random.uniform(jax.random.fold_in(jax.random.fold_in(stream_key, 6), position), (blocks,), jnp.float32, smallest / len(cuts), largest / len(cuts))
        loudness = loudness * jnp.repeat(jnp.exp(draws), dims[position] // blocks).reshape((-1,) + (1,) * (len(dims) - 1 - position))
    return loudness


def noise(rng, shape, spread, most, cuts=(), held_as=jnp.bfloat16):
    drawn = spread * jax.random.normal(rng, shape, jnp.float32)
    if cuts:
        drawn = drawn * levels(rng, shape, cuts, -0.22, 0.18)
    return jnp.clip(drawn, -most, most).astype(held_as)


def setup_inputs(seed: int = 0) -> dict:
    splits = jax.random.split(jax.random.key(seed), 6)
    queries = draw_queries(jax.random.fold_in(splits[5], 71), 0)
    inputs = draw_inputs(jax.random.fold_in(splits[5], 71), 0)
    cotangent = noise(splits[2], (EXAMPLES, L, D), 8.0, 48.0, ((0, 4),))
    key_weight = noise(splits[3], (C, D), C ** -0.5, 0.1875)
    value_weight = noise(splits[4], (C, D), C ** -0.5, 0.1875)
    return {"queries": queries, "inputs": inputs, "cotangent": cotangent, "key_weight": key_weight, "value_weight": value_weight}


def head_grads(query_head, key_head, value_head, cot_head):
    score_scale = 1.0 / jnp.sqrt(jnp.float32(HS))
    scores = jnp.dot(query_head, key_head.T, preferred_element_type=jnp.float32) * score_scale
    row_top = lax.optimization_barrier(jnp.max(scores, axis=-1, keepdims=True))
    expo = jnp.exp(scores - row_top)
    row_total = lax.optimization_barrier(jnp.sum(expo, axis=-1, keepdims=True))
    softmax = expo / row_total
    probability_gradient = jnp.dot(cot_head, value_head.T, preferred_element_type=jnp.float32)
    row_delta = lax.optimization_barrier(jnp.sum(softmax * probability_gradient, axis=-1, keepdims=True))
    score_gradient = (softmax * (probability_gradient - row_delta)).astype(jnp.bfloat16)
    dquery = jnp.dot(score_gradient, key_head, preferred_element_type=jnp.float32) * score_scale
    dkeys = (jnp.dot(score_gradient.T, query_head, preferred_element_type=jnp.float32) * score_scale).astype(jnp.bfloat16)
    softmax_probabilities = softmax.astype(jnp.bfloat16)
    dvalues = jnp.dot(softmax_probabilities.T, cot_head, preferred_element_type=jnp.float32).astype(jnp.bfloat16)
    return (dquery, dkeys, dvalues)

def split_heads(matrix):
    return matrix.reshape(matrix.shape[0], H, HS).transpose(1, 0, 2)

def join_heads(stacked):
    return stacked.transpose(1, 0, 2).reshape(stacked.shape[1], H * HS)

def reference(queries, inputs, cotangent, key_weight, value_weight):

    def one_example(pair):
        features, cot_rows = pair
        key_proj = jnp.dot(features, key_weight, preferred_element_type=jnp.float32).astype(jnp.bfloat16)
        value_proj = jnp.dot(features, value_weight, preferred_element_type=jnp.float32).astype(jnp.bfloat16)

        def per_head(group):
            return head_grads(group[0], group[1], group[2], group[3])
        dquery, dkeys, dvalues = lax.map(per_head, (split_heads(queries), split_heads(key_proj), split_heads(value_proj), split_heads(cot_rows)))
        dkeys = join_heads(dkeys)
        dvalues = join_heads(dvalues)
        grad_in = jnp.dot(dkeys, key_weight.T, preferred_element_type=jnp.float32) + jnp.dot(dvalues, value_weight.T, preferred_element_type=jnp.float32)
        key_part = jnp.dot(features.T, dkeys, preferred_element_type=jnp.float32)
        value_part = jnp.dot(features.T, dvalues, preferred_element_type=jnp.float32)
        return (grad_in.astype(jnp.bfloat16), join_heads(dquery), key_part, value_part)
    grad_in, dquery, key_part, value_part = lax.map(one_example, (inputs, cotangent))
    return (grad_in, lax.optimization_barrier(jnp.sum(dquery, axis=0)), lax.optimization_barrier(jnp.sum(key_part, axis=0)), lax.optimization_barrier(jnp.sum(value_part, axis=0)))
```

```python
import math

import jax
import jax.numpy as jnp
import numpy as np
from jax import lax
from jax.experimental import pallas as pl
from jax.experimental.pallas import tpu as pltpu
from jax.sharding import PartitionSpec as P

L = 512
D = 1024
HS = 128
HD = 4
W = HD * HS
MP = 768
CH = 256
SCALE = 1.0 / math.sqrt(128.0)
EXP2 = SCALE * math.log2(math.e)
BF = jnp.bfloat16
F32 = jnp.float32
AXES = ("seq", "batch")
NT = (((1,), (1,)), ((), ()))
TN = (((0,), (0,)), ((), ()))


def routes(move):
    pairs = []
    for seq in range(64):
        for batch in range(4):
            yl, x, z = seq // 32, seq // 8 % 4, seq % 8
            yh, c = batch // 2, batch % 2
            y, x, z, c = move(yh * 2 + yl, x, z, c)
            y, x, z, c = y % 4, x % 4, z % 8, c % 2
            pairs.append((seq * 4 + batch, (((y % 2) * 4 + x) * 8 + z) * 4 + (y // 2) * 2 + c))
    return pairs


def send(value, move):
    return lax.ppermute(value, AXES, routes(move))


def attend_kernel(pos, x_ref, wk_ref, wv_ref, q_ref, cot_ref, k_ref, e_ref, g_ref, st_ref, s_buf, p_buf):
    x = x_ref[...].astype(BF)
    k = jnp.dot(x, wk_ref[...], preferred_element_type=F32).astype(BF)
    v = jnp.dot(x, wv_ref[...], preferred_element_type=F32).astype(BF)
    k_ref[...] = k
    tops, totals, deltas = [], [], []
    for j in range(2):
        cols = slice(j * HS, (j + 1) * HS)
        kj, vj, qj, cj = k[:, cols], v[:, cols], q_ref[:, cols], cot_ref[:, cols].astype(BF)
        top = jnp.full((8, L), -jnp.inf, F32)
        for r in range(0, MP, CH):
            s = lax.dot_general(kj[r : r + CH], qj, NT, preferred_element_type=F32)
            s_buf[r : r + CH] = s
            p_buf[r : r + CH] = lax.dot_general(vj[r : r + CH], cj, NT, preferred_element_type=F32)
            top = jnp.maximum(top, jnp.max(s.reshape(CH // 8, 8, L), axis=0))
        top = jnp.max(top, axis=0, keepdims=True)
        total = jnp.zeros((8, L), F32)
        delta = jnp.zeros((8, L), F32)
        step = 64
        for r in range(0, MP, step):
            p = jnp.exp2((s_buf[r : r + step] - top) * EXP2)
            dp = p_buf[r : r + step]
            s_buf[r : r + step] = p
            e_ref[r : r + step, j * L : (j + 1) * L] = p.astype(BF)
            total += jnp.sum(p.reshape(step // 8, 8, L), axis=0)
            delta += jnp.sum((p * dp).reshape(step // 8, 8, L), axis=0)
        total = jnp.sum(total, axis=0, keepdims=True)
        delta = jnp.sum(delta, axis=0, keepdims=True)
        mean = delta / total
        for r in range(0, MP, step):
            g_ref[r : r + step, j * L : (j + 1) * L] = (
                s_buf[r : r + step] * (p_buf[r : r + step] - mean)
            ).astype(BF)
        tops.append(top)
        totals.append(total)
        deltas.append(delta)
    st_ref[0] = jnp.concatenate(tops + totals + deltas + [jnp.zeros((2, L), F32)], axis=0)


def attend(pos, x, wk, wv, q, cot, cot_slot):
    mine = lambda g, pos: (0, pos[0] * 2 + g)
    here = lambda g, pos: (0, g)
    return pl.pallas_call(
        attend_kernel,
        grid_spec=pltpu.PrefetchScalarGridSpec(
            num_scalar_prefetch=1,
            grid=(2,),
            in_specs=[
                pl.BlockSpec((MP, D), lambda g, pos: (0, 0)),
                pl.BlockSpec((D, 2 * HS), mine),
                pl.BlockSpec((D, 2 * HS), mine),
                pl.BlockSpec((L, 2 * HS), mine),
                pl.BlockSpec((L, 2 * HS), mine if cot_slot else here),
            ],
            out_specs=[
                pl.BlockSpec((MP, 2 * HS), here),
                pl.BlockSpec((MP, 2 * L), here),
                pl.BlockSpec((MP, 2 * L), here),
                pl.BlockSpec((1, 8, L), lambda g, pos: (g, 0, 0)),
            ],
            scratch_shapes=[pltpu.VMEM((MP, L), F32), pltpu.VMEM((MP, L), F32)],
        ),
        out_shape=[
            jax.ShapeDtypeStruct((MP, W), BF),
            jax.ShapeDtypeStruct((MP, HD * L), BF),
            jax.ShapeDtypeStruct((MP, HD * L), BF),
            jax.ShapeDtypeStruct((2, 8, L), F32),
        ],
        compiler_params=pltpu.CompilerParams(vmem_limit_bytes=40 * 2**20),
        cost_estimate=pl.CostEstimate(flops=3 * 10**9, bytes_accessed=12 * 10**6, transcendentals=10**6),
    )(pos, x, wk, wv, q, cot)


def latent_kernel(e_ref, g_ref, k_ref, ek_ref, gk_ref):
    k = k_ref[...]
    ek_ref[...] = lax.dot_general(e_ref[...], k, TN, preferred_element_type=F32)
    gk_ref[...] = lax.dot_general(g_ref[...], k, TN, preferred_element_type=F32)


def latent_parts(e, g, k):
    at = lambda j: (0, j)
    return pl.pallas_call(
        latent_kernel,
        grid=(HD,),
        in_specs=[pl.BlockSpec((MP, L), at), pl.BlockSpec((MP, L), at), pl.BlockSpec((MP, HS), at)],
        out_specs=[pl.BlockSpec((L, HS), at), pl.BlockSpec((L, HS), at)],
        out_shape=[jax.ShapeDtypeStruct((L, W), F32)] * 2,
        compiler_params=pltpu.CompilerParams(vmem_limit_bytes=24 * 2**20),
        cost_estimate=pl.CostEstimate(flops=10**9, bytes_accessed=8 * 10**6, transcendentals=0),
    )(e, g, k)


def grads_kernel(
    pos, fac_ref, e0_ref, g0_ref, e1_ref, g1_ref, q_ref, c0_ref, c1_ref, x0_ref, x1_ref,
    ek0_ref, gk0_ref, ek1_ref, gk1_ref,
    r0_ref, r1_ref, r2_ref, r3_ref, d0_ref, d1_ref,
    right, left, wg, lat,
):
    i = pl.program_id(0)
    half = MP // CH

    @pl.when(i == 0)
    def _():
        fac = fac_ref[...].T
        for n, (cot_ref, ek_ref, gk_ref) in enumerate(((c0_ref, ek0_ref, gk0_ref), (c1_ref, ek1_ref, gk1_ref))):
            for j in range(HD):
                cols = slice(j * HS, (j + 1) * HS)
                a = fac[:, n * HD + j : n * HD + j + 1]
                eps = fac[:, 8 + n * HD + j : 8 + n * HD + j + 1]
                aq = a * q_ref[:, cols].astype(F32)
                right[n, j, :, :HS] = (eps * aq).astype(BF)
                right[n, j, :, HS:] = (a * cot_ref[:, cols].astype(F32)).astype(BF)
                left[n, j] = aq.astype(BF)
                part = (a * SCALE) * (gk_ref[:, cols] + eps * ek_ref[:, cols])
                rows, at = (j // 2) * L, (j % 2) * HS
                if n == 0:
                    lat[rows : rows + L, at : at + HS] = part
                else:
                    lat[rows : rows + L, at : at + HS] += part

    def chunk(n, e_ref, g_ref, d_ref, r):
        for j in range(HD):
            cols = slice(j * L, (j + 1) * L)
            both = jnp.dot(e_ref[:, cols], right[n, j], preferred_element_type=F32)
            own = jnp.dot(g_ref[:, cols], left[n, j], preferred_element_type=F32)
            d_ref[pl.ds(r, CH), j * HS : (j + 1) * HS] = ((own + both[:, :HS]) * SCALE).astype(BF)
            d_ref[pl.ds(r, CH), W + j * HS : W + (j + 1) * HS] = both[:, HS:].astype(BF)

    @pl.when(i < half)
    def _():
        chunk(0, e0_ref, g0_ref, d0_ref, pl.multiple_of(i * CH, CH))

    @pl.when(i >= half)
    def _():
        chunk(1, e1_ref, g1_ref, d1_ref, pl.multiple_of((i - half) * CH, CH))

    @pl.when(i == 2 * half - 1)
    def _():
        for r in range(0, D, CH):
            for n in range(0, D, CH):
                wg[r : r + CH, n : n + CH] = jnp.dot(
                    x0_ref[r : r + CH], d0_ref[:, n : n + CH], preferred_element_type=F32
                ) + jnp.dot(x1_ref[r : r + CH], d1_ref[:, n : n + CH], preferred_element_type=F32)
        core, mx, my, mz = pos[0], pos[1], pos[2], pos[3]
        m1 = jnp.where(core == 0, mx, my)
        m2 = jnp.where(core == 0, my, mx)
        for r1, out in enumerate((r0_ref, r1_ref, r2_ref, r3_ref)):
            p1 = lax.rem(m1 + r1, 4)

            def place(t, _, p1=p1, out=out):
                p2 = lax.rem(m2 + t // 8, 4)
                z = lax.rem(mz + t % 8, 8)
                x = jnp.where(core == 0, p1, p2)
                y = jnp.where(core == 0, p2, p1)
                s = (y % 2) * 32 + x * 8 + z
                yh = y // 2
                dst = pl.ds(pl.multiple_of(t * 8, 8), 8)
                out[dst, :D] = wg[pl.ds(pl.multiple_of((s * 2 + yh) * 8, 8), 8), :]
                out[dst, D:] = lat[pl.ds(pl.multiple_of(yh * L + s * 8, 8), 8), :]
                return 0

            lax.fori_loop(0, 32, place, 0)


def grads(pos, fac, e0, g0, e1, g1, q, c0, c1, xt0, xt1, ek0, gk0, ek1, gk1):
    half = MP // CH
    first = lambda i, pos: (jnp.minimum(i, half - 1), 0)
    second = lambda i, pos: (jnp.maximum(i - half, 0), 0)
    fixed = lambda i, pos: (0, 0)
    whole = lambda a: pl.BlockSpec(a.shape, fixed)
    mine = lambda i, pos: (0, pos[0])
    return pl.pallas_call(
        grads_kernel,
        grid_spec=pltpu.PrefetchScalarGridSpec(
            num_scalar_prefetch=1,
            grid=(2 * half,),
            in_specs=[
                whole(fac),
                pl.BlockSpec((CH, HD * L), first),
                pl.BlockSpec((CH, HD * L), first),
                pl.BlockSpec((CH, HD * L), second),
                pl.BlockSpec((CH, HD * L), second),
                pl.BlockSpec((L, W), mine),
                pl.BlockSpec((L, W), mine),
                whole(c1),
                whole(xt0),
                whole(xt1),
                whole(ek0),
                whole(gk0),
                whole(ek1),
                whole(gk1),
            ],
            out_specs=[pl.BlockSpec((256, 1280), fixed)] * 4 + [pl.BlockSpec((MP, D), fixed)] * 2,
            scratch_shapes=[
                pltpu.VMEM((2, HD, L, 2 * HS), BF),
                pltpu.VMEM((2, HD, L, HS), BF),
                pltpu.VMEM((D, D), F32),
                pltpu.VMEM((2 * L, 2 * HS), F32),
            ],
        ),
        out_shape=[jax.ShapeDtypeStruct((256, 1280), F32)] * 4 + [jax.ShapeDtypeStruct((MP, D), BF)] * 2,
        compiler_params=pltpu.CompilerParams(vmem_limit_bytes=56 * 2**20),
        cost_estimate=pl.CostEstimate(flops=6 * 10**9, bytes_accessed=26 * 10**6, transcendentals=0),
    )(pos, fac, e0, g0, e1, g1, q, c0, c1, xt0, xt1, ek0, gk0, ek1, gk1)


def merge(parts):
    top = parts[0][:8]
    for p in parts[1:]:
        top = jnp.maximum(top, p[:8])
    total = delta = 0.0
    for p in parts:
        w = jnp.exp2((p[:8] - top) * EXP2)
        total += w * p[8:16]
        delta += w * p[16:]
    return jnp.concatenate([top, total, delta], axis=0)


def body(queries, inputs, cotangent, key_weight, value_weight):
    seq, batch = lax.axis_index("seq"), lax.axis_index("batch")
    yl, mx, mz = seq // 32, seq // 8 % 4, seq % 8
    yh, core = batch // 2, batch % 2
    pos = jnp.stack([core, mx, yh * 2 + yl, mz]).astype(jnp.int32)
    x0, c0 = inputs[0], cotangent[0]

    over = lambda y, x, z, c: (y, x, z, c + 1)
    x1 = send(x0.astype(F32), over)
    c1 = send(lax.dynamic_slice(c0, (0, (1 - core) * W), (L, W)).astype(F32), over)

    k0, e0, g0, st0 = attend(pos, x0, key_weight, value_weight, queries, c0, True)
    k1, e1, g1, st1 = attend(pos, x1, key_weight, value_weight, queries, c1, False)
    local = jnp.concatenate(
        [s[:, r : r + 2].reshape(4, L) for r in (0, 2, 4) for s in (st0, st1)], axis=0
    )
    stats = local
    stats = merge([stats] + [send(stats, lambda y, x, z, c, n=n: (y, x + n, z, c)) for n in (1, 2, 3)])
    stats = merge([stats] + [send(stats, lambda y, x, z, c, n=n: (y, x, z + n, c)) for n in (2, 4, 6)])
    stats = merge(
        [stats]
        + [send(stats, lambda y, x, z, c, n=n: (y ^ (n & 1), x, z ^ (n >> 1), c)) for n in (1, 2, 3)]
    )

    ek0, gk0 = latent_parts(e0, g0, k0)
    ek1, gk1 = latent_parts(e1, g1, k1)
    xt0, xt1 = x0.T, x1.T.astype(BF)
    own_weight = jnp.concatenate(
        [lax.dynamic_slice(w, (0, core * W), (D, W)) for w in (key_weight, value_weight)], axis=1
    )

    a = jnp.exp2((local[:8] - stats[:8]) * EXP2) / stats[8:16]
    eps = local[16:] / local[8:16] - stats[16:] / stats[8:16]
    fac = jnp.concatenate([a, eps], axis=0)
    r0, r1, r2, r3, d0, d1 = grads(
        pos, fac, e0, g0, e1, g1, queries, c0, c1, xt0, xt1, ek0, gk0, ek1, gk1
    )

    def first(n):
        return lambda y, x, z, c: (y, x + n, z, c) if c == 0 else (y + n, x, z, c)

    def second(n):
        return lambda y, x, z, c: (y + n, x, z, c) if c == 0 else (y, x + n, z, c)

    got = [send(r, first(n)) for n, r in ((2, r2), (1, r1), (3, r3))]
    part = [sum((g[64 * n : 64 * n + 64] for g in got), r0[64 * n : 64 * n + 64]) for n in range(4)]
    got = [send(part[n], second(n)) for n in (2, 1, 3)]
    part = [sum((g[16 * n : 16 * n + 16] for g in got), part[0][16 * n : 16 * n + 16]) for n in range(4)]
    got = [send(part[n], lambda y, x, z, c, n=n: (y, x, z + 2 * n, c)) for n in (2, 1, 3)]
    part = [sum((g[8 * n : 8 * n + 8] for g in got), part[0][8 * n : 8 * n + 8]) for n in range(2)]
    mine = part[0] + send(part[1], lambda y, x, z, c: (y, x, z + 1, c))

    theirs = send(mine, over)
    pair = jnp.where(
        core == 0, jnp.concatenate([mine, theirs], axis=1), jnp.concatenate([theirs, mine], axis=1)
    )
    far = send(pair, lambda y, x, z, c: (y + 2, x, z, c))
    low, high = jnp.where(yh == 0, pair, far), jnp.where(yh == 0, far, pair)
    sums = jnp.concatenate([low, high], axis=0)
    key_grad = jnp.concatenate([sums[:, :512], sums[:, 1280:1792]], axis=1)
    value_grad = jnp.concatenate([sums[:, 512:1024], sums[:, 1792:2304]], axis=1)
    latent_grad = jnp.concatenate(
        [low[:, 1024:1280], high[:, 1024:1280], low[:, 2304:], high[:, 2304:]], axis=1
    )

    away = lax.dot_general(d1, own_weight, NT, preferred_element_type=F32)
    home = lax.dot_general(d0, own_weight, NT, preferred_element_type=F32)
    grad_in = (home + send(away, over)).astype(BF)
    return grad_in[None], latent_grad, key_grad, value_grad


def solution(mesh):
    placed = (P(), P("batch", "seq", None), P("batch", None, None), P(), P())
    return jax.shard_map(
        body,
        mesh=mesh,
        in_specs=placed,
        out_specs=(P("batch", "seq", None), P("seq", None), P("seq", None), P("seq", None)),
        check_vma=False,
    )
```

```python
import math

import jax
import jax.numpy as jnp
from jax import lax
from jax.experimental import pallas as pl
from jax.experimental.pallas import tpu as pltpu
from jax.sharding import PartitionSpec as P

L = 512
D = 1024
HS = 128
HD = 4
W = HD * HS
MP = 768
CH = 256
SCALE = 1.0 / math.sqrt(128.0)
EXP2 = SCALE * math.log2(math.e)
BF = jnp.bfloat16
F32 = jnp.float32
AXES = ("seq", "batch")
NT = (((1,), (1,)), ((), ()))
TN = (((0,), (0,)), ((), ()))
VM = pl.BlockSpec(memory_space=pltpu.VMEM)
ANY = pl.BlockSpec(memory_space=pl.ANY)
HOME = 12
LOADL = 52
AWAY = 12
INPUT = 24


def routes(move):
    pairs = []
    for seq in range(64):
        for batch in range(4):
            yl, x, z = seq // 32, seq // 8 % 4, seq % 8
            yh, c = batch // 2, batch % 2
            y, x, z, c = move(yh * 2 + yl, x, z, c)
            y, x, z, c = y % 4, x % 4, z % 8, c % 2
            pairs.append((seq * 4 + batch, (((y % 2) * 4 + x) * 8 + z) * 4 + (y // 2) * 2 + c))
    return pairs


def send(value, move):
    return lax.ppermute(value, AXES, routes(move))


def whole(shape):
    return pl.BlockSpec(shape, lambda i, *_: (0,) * len(shape))


def call(limit, us, kernel, grid, in_specs, out_specs, out_shape, scratch, *args):
    return pl.pallas_call(
        kernel,
        grid_spec=pltpu.PrefetchScalarGridSpec(
            num_scalar_prefetch=1, grid=(grid,), in_specs=in_specs, out_specs=out_specs, scratch_shapes=scratch
        ),
        out_shape=out_shape,
        compiler_params=pltpu.CompilerParams(vmem_limit_bytes=limit * 2**20),
        cost_estimate=pl.CostEstimate(flops=1, bytes_accessed=int(us * 3.6e6), transcendentals=0),
    )(*args)


def project(h, r, x, wk_ref, wv_ref, k_buf, v_buf):
    cols = slice(h * 256, h * 256 + 256)
    k_buf[h, r : r + CH] = jnp.dot(x, wk_ref[:, cols], preferred_element_type=F32).astype(BF)
    v_buf[h, r : r + CH] = jnp.dot(x, wv_ref[:, cols], preferred_element_type=F32).astype(BF)


def attend_heads(q_ref, c_ref, e_ref, g_ref, k_buf, v_buf, s_buf, p_buf, st):
    def multiply(j, r, top):
        h, cols, mine = j // 2, slice(j % 2 * HS, j % 2 * HS + HS), slice(j * HS, j * HS + HS)
        s = lax.dot_general(k_buf[h, r : r + CH, cols], q_ref[:, mine], NT, preferred_element_type=F32)
        s_buf[j % 2, r : r + CH] = s
        p_buf[j % 2, r : r + CH] = lax.dot_general(
            v_buf[h, r : r + CH, cols], c_ref[:, mine], NT, preferred_element_type=F32
        )
        return jnp.maximum(top, jnp.max(s.reshape(CH // 8, 8, L), axis=0))

    def weigh(j, r, top, total, delta):
        for n in range(r, r + CH, 64):
            p = jnp.exp2((s_buf[j % 2, n : n + 64] - top) * EXP2)
            s_buf[j % 2, n : n + 64] = p
            e_ref[j, n : n + 64] = p.astype(BF)
            total += jnp.sum(p.reshape(8, 8, L), axis=0)
            delta += jnp.sum((p * p_buf[j % 2, n : n + 64]).reshape(8, 8, L), axis=0)
        return total, delta

    low = jnp.full((8, L), -jnp.inf, F32)
    zero = jnp.zeros((8, L), F32)
    ahead = low
    for r in range(0, MP, CH):
        ahead = multiply(0, r, ahead)
    for j in range(HD):
        top = jnp.max(ahead, axis=0, keepdims=True)
        total, delta, ahead = zero, zero, low
        for r in range(0, MP, CH):
            if j < HD - 1:
                ahead = multiply(j + 1, r, ahead)
            total, delta = weigh(j, r, top, total, delta)
        total = jnp.sum(total, axis=0, keepdims=True)
        delta = jnp.sum(delta, axis=0, keepdims=True)
        mean = delta / total
        for n in range(0, MP, 64):
            g_ref[j, n : n + 64] = (s_buf[j % 2, n : n + 64] * (p_buf[j % 2, n : n + 64] - mean)).astype(BF)
        st(j, top, total, delta)


def load_kernel(
    pos, x_hbm, wk_hbm, wv_hbm, q_hbm, c_hbm,
    x_ref, wk_ref, wv_ref, q_ref, c_ref, xs_ref, cs_ref,
    cb, sems,
):
    mine = pl.ds(pl.multiple_of(pos[0] * W, W), W)
    theirs = pl.ds(pl.multiple_of((1 - pos[0]) * W, W), W)
    pairs = [(x_hbm.at[pl.ds(n * CH, CH)], x_ref.at[pl.ds(n * CH, CH)]) for n in range(3)]
    pairs += [(c_hbm, cb), (wk_hbm.at[:, mine], wk_ref), (wv_hbm.at[:, mine], wv_ref), (q_hbm.at[:, mine], q_ref)]
    copies = [pltpu.make_async_copy(a, b, sems.at[n]) for n, (a, b) in enumerate(pairs)]
    for c in copies:
        c.start()
    for n in range(3):
        copies[n].wait()
        xs_ref[n * CH : n * CH + CH] = x_ref[n * CH : n * CH + CH].astype(F32)
    copies[3].wait()
    c_ref[...] = cb[:, mine]
    cs_ref[...] = cb[:, theirs].astype(F32)
    for c in copies[4:]:
        c.wait()


PROJ = pltpu.VMEM((2, MP, 256), BF)
MAPS = [pltpu.VMEM((HD, MP, L), BF), pltpu.VMEM((HD, MP, L), BF)]
BUFFERS = [pltpu.VMEM((2, MP, L), F32), pltpu.VMEM((2, MP, L), F32)]


def load(pos, x, wk, wv, q, c):
    return call(
        LOADL, 4, load_kernel, 1, [ANY] * 5, [VM] * 7,
        [
            pltpu.VMEM((MP, D), BF),
            pltpu.VMEM((D, W), BF),
            pltpu.VMEM((D, W), BF),
            pltpu.VMEM((L, W), BF),
            pltpu.VMEM((L, W), BF),
            pltpu.VMEM((MP, D), F32),
            pltpu.VMEM((L, W), F32),
        ],
        [pltpu.VMEM((L, D), BF), pltpu.SemaphoreType.DMA((7,))],
        pos, x, wk, wv, q, c,
    )


def home_kernel(pos, x_ref, wk_ref, wv_ref, q_ref, c_ref, k_ref, e_ref, g_ref, st_ref, v_buf, s_buf, p_buf):
    for h in range(2):
        for r in range(0, MP, CH):
            project(h, r, x_ref[r : r + CH], wk_ref, wv_ref, k_ref, v_buf)

    def st(j, *rows):
        for t, row in enumerate(rows):
            st_ref[t * HD + j : t * HD + j + 1] = row

    attend_heads(q_ref, c_ref, e_ref, g_ref, k_ref, v_buf, s_buf, p_buf, st)


def attend_home(pos, x, wk, wv, q, c):
    return call(
        HOME, 7, home_kernel, 1, [VM] * 5, [VM] * 4, [PROJ, *MAPS, pltpu.VMEM((3 * HD, L), F32)], [PROJ] + BUFFERS,
        pos, x, wk, wv, q, c,
    )


def away_kernel(
    pos, xs_ref, cs_ref, wk_ref, wv_ref, q_ref, st0_ref,
    x_ref, c_ref, k_ref, e_ref, g_ref, st_ref,
    v_buf, s_buf, p_buf,
):
    for n in range(0, MP, CH):
        x = xs_ref[n : n + CH].astype(BF)
        x_ref[n : n + CH] = x
        for h in range(2):
            project(h, n, x, wk_ref, wv_ref, k_ref, v_buf)
    c_ref[...] = cs_ref[...].astype(BF)

    def st(j, *rows):
        for t, row in enumerate(rows):
            st_ref[t * 8 + j : t * 8 + j + 1] = st0_ref[t * HD + j : t * HD + j + 1]
            st_ref[t * 8 + HD + j : t * 8 + HD + j + 1] = row

    attend_heads(q_ref, c_ref, e_ref, g_ref, k_ref, v_buf, s_buf, p_buf, st)


def attend_away(pos, x, c, wk, wv, q, st0):
    return call(
        AWAY, 7, away_kernel, 1, [VM] * 6, [VM] * 6,
        [pltpu.VMEM((MP, D), BF), pltpu.VMEM((L, W), BF), PROJ, *MAPS, pltpu.VMEM((24, L), F32)], [PROJ] + BUFFERS,
        pos, x, c, wk, wv, q, st0,
    )


def merge(parts):
    top = parts[0][:8]
    for p in parts[1:]:
        top = jnp.maximum(top, p[:8])
    total = delta = 0.0
    for p in parts:
        w = jnp.exp2((p[:8] - top) * EXP2)
        total += w * p[8:16]
        delta += w * p[16:24]
    return jnp.concatenate([top, total, delta], axis=0)


def place(core, mx, my, r1, r2):
    p1 = lax.rem(jnp.where(core == 0, mx, my) + r1, 4)
    p2 = lax.rem(jnp.where(core == 0, my, mx) + r2, 4)
    return jnp.where(core == 0, p1, p2), jnp.where(core == 0, p2, p1)


def weight_block(pos, r1, r2, x0_ref, x1_ref, d_ref, out):
    x, y = place(pos[0], pos[1], pos[2], r1, r2)
    rows = pl.ds(pl.multiple_of(((y % 2) * 4 + x) * 128, 128), 128)
    for t in range(2):
        cols = pl.ds(pl.multiple_of(t * W + y // 2 * 256, 256), 256)
        out[:, t * 256 : t * 256 + 256] = lax.dot_general(
            x0_ref[:, rows], d_ref[:MP, cols], TN, preferred_element_type=F32
        ) + lax.dot_general(x1_ref[:, rows], d_ref[MP:, cols], TN, preferred_element_type=F32)


def far_kernel(
    pos, st_ref, p0_ref, p1_ref, p2_ref, p3_ref, e0_ref, g0_ref, e1_ref, g1_ref, q_ref, c0_ref, c1_ref, x0_ref, x1_ref,
    fac_ref, d_ref, away_ref, ra_ref, rb_ref,
    right, left,
):
    local = st_ref[...]
    total = merge([p0_ref[...], p1_ref[...], p2_ref[...], p3_ref[...]])
    a = jnp.exp2((local[:8] - total[:8]) * EXP2) / total[8:16]
    eps = local[16:] / local[8:16] - total[16:] / total[8:16]
    fac = jnp.concatenate([a, eps], axis=0)
    fac_ref[...] = fac
    fac = fac.T
    for n, (e_ref, g_ref, c_ref) in enumerate(((e0_ref, g0_ref, c0_ref), (e1_ref, g1_ref, c1_ref))):
        for j in range(HD):
            cols = slice(j * HS, (j + 1) * HS)
            a = fac[:, n * HD + j : n * HD + j + 1]
            eps = fac[:, 8 + n * HD + j : 8 + n * HD + j + 1]
            aq = a * q_ref[:, cols].astype(F32)
            right[j % 2, :, :HS] = (eps * aq).astype(BF)
            right[j % 2, :, HS:] = (a * c_ref[:, cols].astype(F32)).astype(BF)
            left[j % 2] = aq.astype(BF)
            for r in range(0, MP, CH):
                both = jnp.dot(e_ref[j, r : r + CH], right[j % 2], preferred_element_type=F32)
                own = jnp.dot(g_ref[j, r : r + CH], left[j % 2], preferred_element_type=F32)
                rows = slice(n * MP + r, n * MP + r + CH)
                dk, dv = ((own + both[:, :HS]) * SCALE).astype(BF), both[:, HS:].astype(BF)
                for at, part in ((j * HS, dk), (W + j * HS, dv)):
                    d_ref[rows, at : at + HS] = part
                    if n == 1:
                        away_ref[r : r + CH, at : at + HS] = part.astype(F32)
    for n, (right, left) in enumerate((((2, 0), (2, 2)), ((2, 1), (2, 3)), ((1, 2), (3, 0)), ((1, 3), (3, 1)))):
        weight_block(pos, *right, x0_ref, x1_ref, d_ref, ra_ref.at[n])
        weight_block(pos, *left, x0_ref, x1_ref, d_ref, rb_ref.at[n])


def far_grads(pos, local, parts, e0, g0, e1, g1, q, c0, c1, x0, x1):
    half = pltpu.VMEM((4, 128, 512), F32)
    return call(
        14, 8, far_kernel, 1, [VM] + [whole((24, L))] * 4 + [VM] * 9, [VM] * 5,
        [pltpu.VMEM((16, L), F32), pltpu.VMEM((2 * MP, D), BF), pltpu.VMEM((MP, D), F32), half, half],
        [pltpu.VMEM((2, L, 2 * HS), BF), pltpu.VMEM((2, L, HS), BF)],
        pos, local, *parts, e0, g0, e1, g1, q, c0, c1, x0, x1,
    )


def near_kernel(
    pos, fac_ref, e0_ref, g0_ref, k0_ref, e1_ref, g1_ref, k1_ref, x0_ref, x1_ref, d_ref,
    r0_ref, r1_ref, r3_ref, l0_ref, l1_ref, l2_ref, l3_ref,
    lat,
):
    for n in range(4):
        weight_block(pos, 0, n, x0_ref, x1_ref, d_ref, r0_ref.at[n])
    for n in range(2):
        weight_block(pos, 1, n, x0_ref, x1_ref, d_ref, r1_ref.at[n])
        weight_block(pos, 3, n + 2, x0_ref, x1_ref, d_ref, r3_ref.at[n])
    fac = fac_ref[...].T
    for n, (e_ref, g_ref, k_ref) in enumerate(((e0_ref, g0_ref, k0_ref), (e1_ref, g1_ref, k1_ref))):
        for j in range(HD):
            a = fac[:, n * HD + j : n * HD + j + 1]
            eps = fac[:, 8 + n * HD + j : 8 + n * HD + j + 1]
            k = k_ref[j // 2, :, j % 2 * HS : j % 2 * HS + HS]
            ek = lax.dot_general(e_ref[j], k, TN, preferred_element_type=F32)
            gk = lax.dot_general(g_ref[j], k, TN, preferred_element_type=F32)
            part = (a * SCALE) * (gk + eps * ek)
            at = slice(j % 2 * HS, j % 2 * HS + HS)
            if n == 0:
                lat[j // 2, :, at] = part
            else:
                lat[j // 2, :, at] += part
    core, mx, my = pos[0], pos[1], pos[2]
    for r1, out in enumerate((l0_ref, l1_ref, l2_ref, l3_ref)):
        for r2 in range(4):
            x, y = place(core, mx, my, r1, r2)
            for z in range(8):
                row = pl.multiple_of(((y % 2) * 4 + x) * 64 + z * 8, 8)
                out[r2, z // 2 * 8 : z // 2 * 8 + 8, z % 2 * 256 : z % 2 * 256 + 256] = lat[y // 2, pl.ds(row, 8)]


def near_grads(pos, fac, e0, g0, k0, e1, g1, k1, x0, x1, d):
    block, half, lat = (pltpu.VMEM(shape, F32) for shape in ((4, 128, 512), (2, 128, 512), (4, 32, 512)))
    return call(
        14, 8, near_kernel, 1, [VM] * 10, [VM] * 7, [block, half, half] + [lat] * 4, [pltpu.VMEM((2, L, 2 * HS), F32)],
        pos, fac, e0, g0, k0, e1, g1, k1, x0, x1, d,
    )


def input_kernel(pos, d_ref, wk_ref, wv_ref, got_ref, wk_hbm, wv_hbm, out_ref, wk_buf, wv_buf, total, sems):
    theirs = pl.ds(pl.multiple_of((1 - pos[0]) * W, W), W)
    copies = [
        pltpu.make_async_copy(a.at[:, theirs], b, sems.at[n])
        for n, (a, b) in enumerate(((wk_hbm, wk_buf), (wv_hbm, wv_buf)))
    ]
    for c in copies:
        c.start()
    for r in range(0, MP, CH):
        total[r : r + CH] = lax.dot_general(
            d_ref[r : r + CH, :W], wk_ref[...], NT, preferred_element_type=F32
        ) + lax.dot_general(d_ref[r : r + CH, W:], wv_ref[...], NT, preferred_element_type=F32)
    for c in copies:
        c.wait()
    for r in range(0, MP, CH):
        got = got_ref[r : r + CH].astype(BF)
        out_ref[r : r + CH] = (
            total[r : r + CH]
            + lax.dot_general(got[:, :W], wk_buf[...], NT, preferred_element_type=F32)
            + lax.dot_general(got[:, W:], wv_buf[...], NT, preferred_element_type=F32)
        ).astype(BF)


def input_grads(pos, d, wk, wv, got, key_weight, value_weight):
    return call(
        INPUT, 5.5, input_kernel, 1, [VM] * 4 + [ANY] * 2, [whole((MP, D))], [jax.ShapeDtypeStruct((MP, D), BF)],
        [pltpu.VMEM((D, W), BF), pltpu.VMEM((D, W), BF), pltpu.VMEM((MP, D), F32), pltpu.SemaphoreType.DMA((2,))],
        pos, d, wk, wv, got, key_weight, value_weight,
    )[0]


def fold_kernel(pos, r0_ref, l0_ref, right_ref, left_ref, ra_ref, rb_ref, far_ref, *outs):
    for n, out in enumerate(outs):
        rows = slice(128 * (n % 2), 128 * (n % 2) + 128)
        if n < 2:
            out[:128] = r0_ref[n] + right_ref[rows] + rb_ref[n + 2]
        else:
            out[:128] = r0_ref[n] + left_ref[rows] + ra_ref[n]
        lat = slice(256 + 32 * n, 288 + 32 * n)
        out[128:] = l0_ref[n] + far_ref[n] + right_ref[lat] + left_ref[lat]


def fold(pos, *args):
    return call(8, 0.5, fold_kernel, 1, [VM] * 7, [VM] * 4, [pltpu.VMEM((160, 512), F32)] * 4, [], pos, *args)


def turn_kernel(pos, a_ref, b_ref, c_ref, d_ref, *outs):
    outs[4][...] = a_ref[...] + b_ref[...] + c_ref[...] + d_ref[...]
    for r in range(8):
        z = lax.rem(pos[3] + r, 8)
        out = outs[r // 2]
        out[r % 2 * 16 : r % 2 * 16 + 16] = outs[4][pl.ds(pl.multiple_of(z * 16, 16), 16)]
        rows = outs[4][pl.ds(pl.multiple_of(128 + z // 2 * 8, 8), 8)]
        out[32:40, r % 2 * 256 : r % 2 * 256 + 256] = jnp.where(z % 2 == 0, rows[:, :256], rows[:, 256:])


def turn(pos, parts):
    return call(
        8, 0.7, turn_kernel, 1, [VM] * 4, [VM] * 4, [pltpu.VMEM((40, 512), F32)] * 4,
        [pltpu.VMEM((160, 512), F32)], pos, *parts,
    )


def finish_kernel(pos, mine_ref, other_ref, latent_ref, key_ref, value_ref):
    for c in range(2):
        src = jnp.where(pos[0] == c, mine_ref[...], other_ref[...])
        for y in range(2):
            to, at = slice(c * W + y * 256, c * W + y * 256 + 256), y * 768
            key_ref[:, to] = src[:, at : at + 256]
            value_ref[:, to] = src[:, at + 256 : at + 512]
            latent_ref[:, to] = src[:8, at + 512 : at + 768]


def body(queries, inputs, cotangent, key_weight, value_weight):
    seq, batch = lax.axis_index("seq"), lax.axis_index("batch")
    yl, mx, mz = seq // 32, seq // 8 % 4, seq % 8
    yh, core = batch // 2, batch % 2
    pos = jnp.stack([core, mx, yh * 2 + yl, mz]).astype(jnp.int32)

    over = lambda y, x, z, c: (y, x, z, c + 1)
    x0, wk, wv, q, c0, xs, cs = load(pos, inputs[0], key_weight, value_weight, queries, cotangent[0])
    xs, cs = send(xs, over), send(cs, over)
    k0, e0, g0, st0 = attend_home(pos, x0, wk, wv, q, c0)
    x1, c1, k1, e1, g1, local = attend_away(pos, xs, cs, wk, wv, q, st0)

    stats = local
    stats = merge([stats] + [send(stats, lambda y, x, z, c, n=n: (y, x + n, z, c)) for n in (1, 2, 3)])
    stats = merge([stats] + [send(stats, lambda y, x, z, c, n=n: (y, x, z + n, c)) for n in (2, 4, 6)])
    parts = [stats] + [
        send(stats, lambda y, x, z, c, n=n: (y ^ (n & 1), x, z ^ (n >> 1), c)) for n in (1, 2, 3)
    ]

    fac, d, back, ra, rb = far_grads(pos, local, parts, e0, g0, e1, g1, q, c0, c1, x0, x1)

    def first(n):
        return lambda y, x, z, c: (y, x + n, z, c) if c == 0 else (y + n, x, z, c)

    def second(n):
        return lambda y, x, z, c: (y + n, x, z, c) if c == 0 else (y, x + n, z, c)

    ra, rb = send(ra, first(1)), send(rb, first(-1))
    r0, r1, r3, l0, l1, l2, l3 = near_grads(pos, fac, e0, g0, k0, e1, g1, k1, x0, x1, d)
    back, r0 = lax.optimization_barrier((back, r0))
    back = send(back, over)
    right = jnp.concatenate([(r1 + ra[:2]).reshape(256, 512), l1.reshape(128, 512)], axis=0)
    left = jnp.concatenate([(r3 + rb[:2]).reshape(256, 512), l3.reshape(128, 512)], axis=0)
    d, right_buf, left_buf = lax.optimization_barrier((d, right, left))
    right, left, far_l = send(right, first(1)), send(left, first(-1)), send(l2, first(2))
    grad_in = input_grads(pos, d, wk, wv, back, key_weight, value_weight)
    r0, grad_in = lax.optimization_barrier((r0, grad_in))
    parts = fold(pos, r0, l0, right, left, ra, rb, far_l)
    parts = turn(pos, [parts[0]] + [send(parts[n], second(n)) for n in (2, 1, 3)])
    parts = [parts[0]] + [send(parts[n], lambda y, x, z, c, n=n: (y, x, z + 2 * n, c)) for n in (2, 1, 3)]
    total = parts[0] + parts[1] + parts[2] + parts[3]
    here = jnp.concatenate([total[:16], jnp.concatenate([total[32:, :256], jnp.zeros((8, 256), F32)], 0)], axis=1)
    next_z = jnp.concatenate([total[16:32], jnp.concatenate([total[32:, 256:], jnp.zeros((8, 256), F32)], 0)], axis=1)
    near = here + send(next_z, lambda y, x, z, c: (y, x, z + 1, c))
    far = send(here, lambda y, x, z, c: (y + 2, x, z, c)) + send(next_z, lambda y, x, z, c: (y + 2, x, z + 1, c))
    pair = jnp.where(yh == 0, jnp.concatenate([near, far], axis=1), jnp.concatenate([far, near], axis=1))
    other = send(pair, over)
    latent_grad, key_grad, value_grad = call(
        8, 0.7, finish_kernel, 1, [whole((16, 1536))] * 2, [whole((8, D)), whole((16, D)), whole((16, D))],
        [jax.ShapeDtypeStruct((8, D), F32)] + [jax.ShapeDtypeStruct((16, D), F32)] * 2, [], pos, pair, other,
    )
    return grad_in[None], latent_grad, key_grad, value_grad


def solution(mesh):
    placed = (P(), P("batch", "seq", None), P("batch", None, None), P(), P())
    return jax.shard_map(
        body,
        mesh=mesh,
        in_specs=placed,
        out_specs=(P("batch", "seq", None), P("seq", None), P("seq", None), P("seq", None)),
        check_vma=False,
    )
```

```python
import math

import jax
import jax.numpy as jnp
from jax import lax
from jax.experimental import pallas as pl
from jax.experimental.pallas import tpu as pltpu
from jax.sharding import PartitionSpec as P

L = 512
D = 1024
HS = 128
HD = 4
W = HD * HS
MP = 768
CH = 256
SCALE = 1.0 / math.sqrt(128.0)
EXP2 = SCALE * math.log2(math.e)
BF = jnp.bfloat16
F32 = jnp.float32
AXES = ("seq", "batch")
NT = (((1,), (1,)), ((), ()))
TN = (((0,), (0,)), ((), ()))
VM = pl.BlockSpec(memory_space=pltpu.VMEM)
ANY = pl.BlockSpec(memory_space=pl.ANY)
HOME = 12
LOADL = 52
AWAY = 12
INPUT = 24


def routes(move):
    pairs = []
    for seq in range(64):
        for batch in range(4):
            yl, x, z = seq // 32, seq // 8 % 4, seq % 8
            yh, c = batch // 2, batch % 2
            y, x, z, c = move(yh * 2 + yl, x, z, c)
            y, x, z, c = y % 4, x % 4, z % 8, c % 2
            pairs.append((seq * 4 + batch, (((y % 2) * 4 + x) * 8 + z) * 4 + (y // 2) * 2 + c))
    return pairs


def send(value, move):
    return lax.ppermute(value, AXES, routes(move))


def whole(shape):
    return pl.BlockSpec(shape, lambda i, *_: (0,) * len(shape))


def call(limit, us, kernel, grid, in_specs, out_specs, out_shape, scratch, *args):
    return pl.pallas_call(
        kernel,
        grid_spec=pltpu.PrefetchScalarGridSpec(
            num_scalar_prefetch=1, grid=(grid,), in_specs=in_specs, out_specs=out_specs, scratch_shapes=scratch
        ),
        out_shape=out_shape,
        compiler_params=pltpu.CompilerParams(vmem_limit_bytes=limit * 2**20),
        cost_estimate=pl.CostEstimate(flops=1, bytes_accessed=int(us * 3.6e6), transcendentals=0),
    )(*args)


def project(h, r, x, wk_ref, wv_ref, k_buf, v_buf):
    cols = slice(h * 256, h * 256 + 256)
    k_buf[h, r : r + CH] = jnp.dot(x, wk_ref[:, cols], preferred_element_type=F32).astype(BF)
    v_buf[h, r : r + CH] = jnp.dot(x, wv_ref[:, cols], preferred_element_type=F32).astype(BF)


def attend_heads(q_ref, c_ref, e_ref, g_ref, k_buf, v_buf, s_buf, p_buf, st):
    def multiply(j, r, top):
        h, cols, mine = j // 2, slice(j % 2 * HS, j % 2 * HS + HS), slice(j * HS, j * HS + HS)
        s = lax.dot_general(k_buf[h, r : r + CH, cols], q_ref[:, mine], NT, preferred_element_type=F32)
        s_buf[j % 2, r : r + CH] = s
        p_buf[j % 2, r : r + CH] = lax.dot_general(
            v_buf[h, r : r + CH, cols], c_ref[:, mine], NT, preferred_element_type=F32
        )
        return jnp.maximum(top, jnp.max(s.reshape(CH // 8, 8, L), axis=0))

    def weigh(j, r, top, total, delta):
        for n in range(r, r + CH, 64):
            p = jnp.exp2((s_buf[j % 2, n : n + 64] - top) * EXP2)
            s_buf[j % 2, n : n + 64] = p
            e_ref[j, n : n + 64] = p.astype(BF)
            total += jnp.sum(p.reshape(8, 8, L), axis=0)
            delta += jnp.sum((p * p_buf[j % 2, n : n + 64]).reshape(8, 8, L), axis=0)
        return total, delta

    low = jnp.full((8, L), -jnp.inf, F32)
    zero = jnp.zeros((8, L), F32)
    ahead = low
    for r in range(0, MP, CH):
        ahead = multiply(0, r, ahead)
    for j in range(HD):
        top = jnp.max(ahead, axis=0, keepdims=True)
        total, delta, ahead = zero, zero, low
        for r in range(0, MP, CH):
            if j < HD - 1:
                ahead = multiply(j + 1, r, ahead)
            total, delta = weigh(j, r, top, total, delta)
        total = jnp.sum(total, axis=0, keepdims=True)
        delta = jnp.sum(delta, axis=0, keepdims=True)
        mean = delta / total
        for n in range(0, MP, 64):
            g_ref[j, n : n + 64] = (s_buf[j % 2, n : n + 64] * (p_buf[j % 2, n : n + 64] - mean)).astype(BF)
        st(j, top, total, delta)


def load_kernel(
    pos, x_hbm, wk_hbm, wv_hbm, q_hbm, c_hbm,
    x_ref, wk_ref, wv_ref, q_ref, c_ref, xs_ref, cs_ref,
    cb, sems,
):
    mine = pl.ds(pl.multiple_of(pos[0] * W, W), W)
    theirs = pl.ds(pl.multiple_of((1 - pos[0]) * W, W), W)
    pairs = [(x_hbm.at[pl.ds(n * CH, CH)], x_ref.at[pl.ds(n * CH, CH)]) for n in range(3)]
    pairs += [(c_hbm, cb), (wk_hbm.at[:, mine], wk_ref), (wv_hbm.at[:, mine], wv_ref), (q_hbm.at[:, mine], q_ref)]
    copies = [pltpu.make_async_copy(a, b, sems.at[n]) for n, (a, b) in enumerate(pairs)]
    for c in copies:
        c.start()
    for n in range(3):
        copies[n].wait()
        xs_ref[n * CH : n * CH + CH] = x_ref[n * CH : n * CH + CH].astype(F32)
    copies[3].wait()
    c_ref[...] = cb[:, mine]
    cs_ref[...] = cb[:, theirs].astype(F32)
    for c in copies[4:]:
        c.wait()


PROJ = pltpu.VMEM((2, MP, 256), BF)
MAPS = [pltpu.VMEM((HD, MP, L), BF), pltpu.VMEM((HD, MP, L), BF)]
BUFFERS = [pltpu.VMEM((2, MP, L), F32), pltpu.VMEM((2, MP, L), F32)]


def load(pos, x, wk, wv, q, c):
    return call(
        LOADL, 4, load_kernel, 1, [ANY] * 5, [VM] * 7,
        [
            pltpu.VMEM((MP, D), BF),
            pltpu.VMEM((D, W), BF),
            pltpu.VMEM((D, W), BF),
            pltpu.VMEM((L, W), BF),
            pltpu.VMEM((L, W), BF),
            pltpu.VMEM((MP, D), F32),
            pltpu.VMEM((L, W), F32),
        ],
        [pltpu.VMEM((L, D), BF), pltpu.SemaphoreType.DMA((7,))],
        pos, x, wk, wv, q, c,
    )


def home_kernel(pos, x_ref, wk_ref, wv_ref, q_ref, c_ref, k_ref, e_ref, g_ref, st_ref, v_buf, s_buf, p_buf):
    for h in range(2):
        for r in range(0, MP, CH):
            project(h, r, x_ref[r : r + CH], wk_ref, wv_ref, k_ref, v_buf)

    def st(j, *rows):
        for t, row in enumerate(rows):
            st_ref[t * HD + j : t * HD + j + 1] = row

    attend_heads(q_ref, c_ref, e_ref, g_ref, k_ref, v_buf, s_buf, p_buf, st)


def attend_home(pos, x, wk, wv, q, c):
    return call(
        HOME, 7, home_kernel, 1, [VM] * 5, [VM] * 4, [PROJ, *MAPS, pltpu.VMEM((3 * HD, L), F32)], [PROJ] + BUFFERS,
        pos, x, wk, wv, q, c,
    )


def away_kernel(
    pos, xs_ref, cs_ref, wk_ref, wv_ref, q_ref, st0_ref,
    x_ref, c_ref, k_ref, e_ref, g_ref, st_ref,
    v_buf, s_buf, p_buf,
):
    for n in range(0, MP, CH):
        x = xs_ref[n : n + CH].astype(BF)
        x_ref[n : n + CH] = x
        for h in range(2):
            project(h, n, x, wk_ref, wv_ref, k_ref, v_buf)
    c_ref[...] = cs_ref[...].astype(BF)

    def st(j, *rows):
        for t, row in enumerate(rows):
            st_ref[t * 8 + j : t * 8 + j + 1] = st0_ref[t * HD + j : t * HD + j + 1]
            st_ref[t * 8 + HD + j : t * 8 + HD + j + 1] = row

    attend_heads(q_ref, c_ref, e_ref, g_ref, k_ref, v_buf, s_buf, p_buf, st)


def attend_away(pos, x, c, wk, wv, q, st0):
    return call(
        AWAY, 7, away_kernel, 1, [VM] * 6, [VM] * 6,
        [pltpu.VMEM((MP, D), BF), pltpu.VMEM((L, W), BF), PROJ, *MAPS, pltpu.VMEM((24, L), F32)], [PROJ] + BUFFERS,
        pos, x, c, wk, wv, q, st0,
    )


def merge(parts):
    top = parts[0][:8]
    for p in parts[1:]:
        top = jnp.maximum(top, p[:8])
    total = delta = 0.0
    for p in parts:
        w = jnp.exp2((p[:8] - top) * EXP2)
        total += w * p[8:16]
        delta += w * p[16:24]
    return jnp.concatenate([top, total, delta], axis=0)


def place(core, mx, my, r1, r2):
    p1 = lax.rem(jnp.where(core == 0, mx, my) + r1, 4)
    p2 = lax.rem(jnp.where(core == 0, my, mx) + r2, 4)
    return jnp.where(core == 0, p1, p2), jnp.where(core == 0, p2, p1)


def weight_block(pos, r1, r2, x0_ref, x1_ref, d_ref, out):
    x, y = place(pos[0], pos[1], pos[2], r1, r2)
    rows = pl.ds(pl.multiple_of(((y % 2) * 4 + x) * 128, 128), 128)
    for t in range(2):
        cols = pl.ds(pl.multiple_of(t * W + y // 2 * 256, 256), 256)
        out[:, t * 256 : t * 256 + 256] = lax.dot_general(
            x0_ref[:, rows], d_ref[:MP, cols], TN, preferred_element_type=F32
        ) + lax.dot_general(x1_ref[:, rows], d_ref[MP:, cols], TN, preferred_element_type=F32)


def far_kernel(
    pos, st_ref, p0_ref, p1_ref, p2_ref, p3_ref, e0_ref, g0_ref, e1_ref, g1_ref, q_ref, c0_ref, c1_ref, x0_ref, x1_ref,
    fac_ref, d_ref, away_ref, ra_ref, rb_ref,
    right, left,
):
    local = st_ref[...]
    total = merge([p0_ref[...], p1_ref[...], p2_ref[...], p3_ref[...]])
    a = jnp.exp2((local[:8] - total[:8]) * EXP2) / total[8:16]
    eps = local[16:] / local[8:16] - total[16:] / total[8:16]
    fac = jnp.concatenate([a, eps], axis=0)
    fac_ref[...] = fac
    fac = fac.T
    for n, (e_ref, g_ref, c_ref) in enumerate(((e0_ref, g0_ref, c0_ref), (e1_ref, g1_ref, c1_ref))):
        for j in range(HD):
            cols = slice(j * HS, (j + 1) * HS)
            a = fac[:, n * HD + j : n * HD + j + 1]
            eps = fac[:, 8 + n * HD + j : 8 + n * HD + j + 1]
            aq = a * q_ref[:, cols].astype(F32)
            right[j % 2, :, :HS] = (eps * aq).astype(BF)
            right[j % 2, :, HS:] = (a * c_ref[:, cols].astype(F32)).astype(BF)
            left[j % 2] = aq.astype(BF)
            for r in range(0, MP, CH):
                both = jnp.dot(e_ref[j, r : r + CH], right[j % 2], preferred_element_type=F32)
                own = jnp.dot(g_ref[j, r : r + CH], left[j % 2], preferred_element_type=F32)
                rows = slice(n * MP + r, n * MP + r + CH)
                dk, dv = ((own + both[:, :HS]) * SCALE).astype(BF), both[:, HS:].astype(BF)
                for at, part in ((j * HS, dk), (W + j * HS, dv)):
                    d_ref[rows, at : at + HS] = part
                    if n == 1:
                        away_ref[r : r + CH, at : at + HS] = part.astype(F32)
    for n, (right, left) in enumerate((((2, 0), (2, 2)), ((2, 1), (2, 3)), ((1, 2), (3, 0)), ((1, 3), (3, 1)))):
        weight_block(pos, *right, x0_ref, x1_ref, d_ref, ra_ref.at[n])
        weight_block(pos, *left, x0_ref, x1_ref, d_ref, rb_ref.at[n])


def far_grads(pos, local, parts, e0, g0, e1, g1, q, c0, c1, x0, x1):
    half = pltpu.VMEM((4, 128, 512), F32)
    return call(
        14, 8, far_kernel, 1, [VM] + [whole((24, L))] * 4 + [VM] * 9, [VM] * 5,
        [pltpu.VMEM((16, L), F32), pltpu.VMEM((2 * MP, D), BF), pltpu.VMEM((MP, D), F32), half, half],
        [pltpu.VMEM((2, L, 2 * HS), BF), pltpu.VMEM((2, L, HS), BF)],
        pos, local, *parts, e0, g0, e1, g1, q, c0, c1, x0, x1,
    )


def near_kernel(
    pos, fac_ref, e0_ref, g0_ref, k0_ref, e1_ref, g1_ref, k1_ref, x0_ref, x1_ref, d_ref,
    r0_ref, r1_ref, r3_ref, l0_ref, l1_ref, l2_ref, l3_ref,
    lat,
):

    def block(n, _):
        weight_block(pos, 0, n, x0_ref, x1_ref, d_ref, r0_ref.at[n])
        weight_block(pos, 0, n + 2, x0_ref, x1_ref, d_ref, r0_ref.at[n + 2])
        weight_block(pos, 1, n, x0_ref, x1_ref, d_ref, r1_ref.at[n])
        weight_block(pos, 3, n + 2, x0_ref, x1_ref, d_ref, r3_ref.at[n])
        return 0

    lax.fori_loop(0, 2, block, 0)
    fac = fac_ref[...].T
    for n, (e_ref, g_ref, k_ref) in enumerate(((e0_ref, g0_ref, k0_ref), (e1_ref, g1_ref, k1_ref))):
        for j in range(HD):
            a = fac[:, n * HD + j : n * HD + j + 1]
            eps = fac[:, 8 + n * HD + j : 8 + n * HD + j + 1]
            k = k_ref[j // 2, :, j % 2 * HS : j % 2 * HS + HS]
            ek = lax.dot_general(e_ref[j], k, TN, preferred_element_type=F32)
            gk = lax.dot_general(g_ref[j], k, TN, preferred_element_type=F32)
            part = (a * SCALE) * (gk + eps * ek)
            at = slice(j % 2 * HS, j % 2 * HS + HS)
            if n == 0:
                lat[j // 2, :, at] = part
            else:
                lat[j // 2, :, at] += part
    core, mx, my = pos[0], pos[1], pos[2]
    for r1, out in enumerate((l0_ref, l1_ref, l2_ref, l3_ref)):
        for r2 in range(4):
            x, y = place(core, mx, my, r1, r2)
            for z in range(8):
                row = pl.multiple_of(((y % 2) * 4 + x) * 64 + z * 8, 8)
                out[r2, z // 2 * 8 : z // 2 * 8 + 8, z % 2 * 256 : z % 2 * 256 + 256] = lat[y // 2, pl.ds(row, 8)]


def near_grads(pos, fac, e0, g0, k0, e1, g1, k1, x0, x1, d):
    block, half, lat = (pltpu.VMEM(shape, F32) for shape in ((4, 128, 512), (2, 128, 512), (4, 32, 512)))
    return call(
        14, 8, near_kernel, 1, [VM] * 10, [VM] * 7, [block, half, half] + [lat] * 4, [pltpu.VMEM((2, L, 2 * HS), F32)],
        pos, fac, e0, g0, k0, e1, g1, k1, x0, x1, d,
    )


def input_kernel(pos, d_ref, wk_ref, wv_ref, got_ref, wk_hbm, wv_hbm, out_ref, wk_buf, wv_buf, total, sems):
    theirs = pl.ds(pl.multiple_of((1 - pos[0]) * W, W), W)
    copies = [
        pltpu.make_async_copy(a.at[:, theirs], b, sems.at[n])
        for n, (a, b) in enumerate(((wk_hbm, wk_buf), (wv_hbm, wv_buf)))
    ]
    for c in copies:
        c.start()
    for r in range(0, MP, CH):
        total[r : r + CH] = lax.dot_general(
            d_ref[r : r + CH, :W], wk_ref[...], NT, preferred_element_type=F32
        ) + lax.dot_general(d_ref[r : r + CH, W:], wv_ref[...], NT, preferred_element_type=F32)
    for c in copies:
        c.wait()
    for r in range(0, MP, CH):
        got = got_ref[r : r + CH].astype(BF)
        out_ref[r : r + CH] = (
            total[r : r + CH]
            + lax.dot_general(got[:, :W], wk_buf[...], NT, preferred_element_type=F32)
            + lax.dot_general(got[:, W:], wv_buf[...], NT, preferred_element_type=F32)
        ).astype(BF)


def input_grads(pos, d, wk, wv, got, key_weight, value_weight):
    return call(
        INPUT, 5.5, input_kernel, 1, [VM] * 4 + [ANY] * 2, [whole((MP, D))], [jax.ShapeDtypeStruct((MP, D), BF)],
        [pltpu.VMEM((D, W), BF), pltpu.VMEM((D, W), BF), pltpu.VMEM((MP, D), F32), pltpu.SemaphoreType.DMA((2,))],
        pos, d, wk, wv, got, key_weight, value_weight,
    )[0]


def fold_kernel(pos, r0_ref, l0_ref, right_ref, left_ref, ra_ref, rb_ref, far_ref, *outs):
    for n, out in enumerate(outs):
        rows = slice(128 * (n % 2), 128 * (n % 2) + 128)
        if n < 2:
            out[:128] = r0_ref[n] + right_ref[rows] + rb_ref[n + 2]
        else:
            out[:128] = r0_ref[n] + left_ref[rows] + ra_ref[n]
        lat = slice(256 + 32 * n, 288 + 32 * n)
        out[128:] = l0_ref[n] + far_ref[n] + right_ref[lat] + left_ref[lat]


def fold(pos, *args):
    return call(8, 0.5, fold_kernel, 1, [VM] * 7, [VM] * 4, [pltpu.VMEM((160, 512), F32)] * 4, [], pos, *args)


def turn_kernel(pos, a_ref, b_ref, c_ref, d_ref, *outs):
    outs[4][...] = a_ref[...] + b_ref[...] + c_ref[...] + d_ref[...]
    for r in range(8):
        z = lax.rem(pos[3] + r, 8)
        out = outs[r // 2]
        out[r % 2 * 16 : r % 2 * 16 + 16] = outs[4][pl.ds(pl.multiple_of(z * 16, 16), 16)]
        rows = outs[4][pl.ds(pl.multiple_of(128 + z // 2 * 8, 8), 8)]
        out[32:40, r % 2 * 256 : r % 2 * 256 + 256] = jnp.where(z % 2 == 0, rows[:, :256], rows[:, 256:])


def turn(pos, parts):
    return call(
        8, 0.7, turn_kernel, 1, [VM] * 4, [VM] * 4, [pltpu.VMEM((40, 512), F32)] * 4,
        [pltpu.VMEM((160, 512), F32)], pos, *parts,
    )


def body(queries, inputs, cotangent, key_weight, value_weight):
    seq, batch = lax.axis_index("seq"), lax.axis_index("batch")
    yl, mx, mz = seq // 32, seq // 8 % 4, seq % 8
    yh, core = batch // 2, batch % 2
    pos = jnp.stack([core, mx, yh * 2 + yl, mz]).astype(jnp.int32)

    over = lambda y, x, z, c: (y, x, z, c + 1)
    x0, wk, wv, q, c0, xs, cs = load(pos, inputs[0], key_weight, value_weight, queries, cotangent[0])
    xs, cs = send(xs, over), send(cs, over)
    k0, e0, g0, st0 = attend_home(pos, x0, wk, wv, q, c0)
    x1, c1, k1, e1, g1, local = attend_away(pos, xs, cs, wk, wv, q, st0)

    stats = local
    stats = merge([stats] + [send(stats, lambda y, x, z, c, n=n: (y, x + n, z, c)) for n in (1, 2, 3)])
    stats = merge([stats] + [send(stats, lambda y, x, z, c, n=n: (y, x, z + n, c)) for n in (2, 4, 6)])
    parts = [stats] + [
        send(stats, lambda y, x, z, c, n=n: (y ^ (n & 1), x, z ^ (n >> 1), c)) for n in (1, 2, 3)
    ]

    fac, d, back, ra, rb = far_grads(pos, local, parts, e0, g0, e1, g1, q, c0, c1, x0, x1)

    def first(n):
        return lambda y, x, z, c: (y, x + n, z, c) if c == 0 else (y + n, x, z, c)

    def second(n):
        return lambda y, x, z, c: (y + n, x, z, c) if c == 0 else (y, x + n, z, c)

    ra, rb = send(ra, first(1)), send(rb, first(-1))
    r0, r1, r3, l0, l1, l2, l3 = near_grads(pos, fac, e0, g0, k0, e1, g1, k1, x0, x1, d)
    back = send(back, over)
    right = jnp.concatenate([(r1 + ra[:2]).reshape(256, 512), l1.reshape(128, 512)], axis=0)
    left = jnp.concatenate([(r3 + rb[:2]).reshape(256, 512), l3.reshape(128, 512)], axis=0)
    d, right_buf, left_buf = lax.optimization_barrier((d, right, left))
    right, left, far_l = send(right, first(1)), send(left, first(-1)), send(l2, first(2))
    grad_in = input_grads(pos, d, wk, wv, back, key_weight, value_weight)
    r0, grad_in = lax.optimization_barrier((r0, grad_in))
    parts = fold(pos, r0, l0, right, left, ra, rb, far_l)
    parts = turn(pos, [parts[0]] + [send(parts[n], second(n)) for n in (2, 1, 3)])
    parts = [parts[0]] + [send(parts[n], lambda y, x, z, c, n=n: (y, x, z + 2 * n, c)) for n in (2, 1, 3)]
    total = parts[0] + parts[1] + parts[2] + parts[3]
    here = jnp.concatenate([total[:16], jnp.concatenate([total[32:, :256], jnp.zeros((8, 256), F32)], 0)], axis=1)
    next_z = jnp.concatenate([total[16:32], jnp.concatenate([total[32:, 256:], jnp.zeros((8, 256), F32)], 0)], axis=1)
    near = here + send(next_z, lambda y, x, z, c: (y, x, z + 1, c))
    far = send(here, lambda y, x, z, c: (y + 2, x, z, c)) + send(next_z, lambda y, x, z, c: (y + 2, x, z + 1, c))
    pair = jnp.where(yh == 0, jnp.concatenate([near, far], axis=1), jnp.concatenate([far, near], axis=1))
    other = send(pair, over)
    low, high = jnp.where(core == 0, pair, other), jnp.where(core == 0, other, pair)

    def pick(start, stop, rows):
        return jnp.concatenate([a[:rows, b + start : b + stop] for a in (low, high) for b in (0, 768)], axis=1)

    return grad_in[None], pick(512, 768, 8), pick(0, 256, 16), pick(256, 512, 16)


def solution(mesh):
    placed = (P(), P("batch", "seq", None), P("batch", None, None), P(), P())
    return jax.shard_map(
        body,
        mesh=mesh,
        in_specs=placed,
        out_specs=(P("batch", "seq", None), P("seq", None), P("seq", None), P("seq", None)),
        check_vma=False,
    )
```

```python
import math

import jax
import jax.numpy as jnp
from jax import lax
from jax.experimental import pallas as pl
from jax.experimental.pallas import tpu as pltpu
from jax.sharding import PartitionSpec as P

L = 512
D = 1024
HS = 128
HD = 4
W = HD * HS
MP = 768
CH = 256
SCALE = 1.0 / math.sqrt(128.0)
EXP2 = SCALE * math.log2(math.e)
BF = jnp.bfloat16
F32 = jnp.float32
AXES = ("seq", "batch")
NT = (((1,), (1,)), ((), ()))
TN = (((0,), (0,)), ((), ()))
VM = pl.BlockSpec(memory_space=pltpu.VMEM)
ANY = pl.BlockSpec(memory_space=pl.ANY)
HOME = 12
LOADL = 52
AWAY = 12
INPUT = 24


def routes(move):
    pairs = []
    for seq in range(64):
        for batch in range(4):
            yl, x, z = seq // 32, seq // 8 % 4, seq % 8
            yh, c = batch // 2, batch % 2
            y, x, z, c = move(yh * 2 + yl, x, z, c)
            y, x, z, c = y % 4, x % 4, z % 8, c % 2
            pairs.append((seq * 4 + batch, (((y % 2) * 4 + x) * 8 + z) * 4 + (y // 2) * 2 + c))
    return pairs


def send(value, move):
    return lax.ppermute(value, AXES, routes(move))


def whole(shape):
    return pl.BlockSpec(shape, lambda i, *_: (0,) * len(shape))


def call(limit, us, kernel, grid, in_specs, out_specs, out_shape, scratch, *args):
    return pl.pallas_call(
        kernel,
        grid_spec=pltpu.PrefetchScalarGridSpec(
            num_scalar_prefetch=1, grid=(grid,), in_specs=in_specs, out_specs=out_specs, scratch_shapes=scratch
        ),
        out_shape=out_shape,
        compiler_params=pltpu.CompilerParams(vmem_limit_bytes=limit * 2**20),
        cost_estimate=pl.CostEstimate(flops=1, bytes_accessed=int(us * 3.6e6), transcendentals=0),
    )(*args)


def project(h, r, x, wk_ref, wv_ref, k_buf, v_buf):
    cols = slice(h * 256, h * 256 + 256)
    k_buf[h, r : r + CH] = jnp.dot(x, wk_ref[:, cols], preferred_element_type=F32).astype(BF)
    v_buf[h, r : r + CH] = jnp.dot(x, wv_ref[:, cols], preferred_element_type=F32).astype(BF)


def attend_heads(q_ref, c_ref, e_ref, g_ref, k_buf, v_buf, s_buf, p_buf, st):
    def multiply(j, r, top):
        h, cols, mine = j // 2, slice(j % 2 * HS, j % 2 * HS + HS), slice(j * HS, j * HS + HS)
        s = lax.dot_general(k_buf[h, r : r + CH, cols], q_ref[:, mine], NT, preferred_element_type=F32)
        s_buf[j % 2, r : r + CH] = s
        p_buf[j % 2, r : r + CH] = lax.dot_general(
            v_buf[h, r : r + CH, cols], c_ref[:, mine], NT, preferred_element_type=F32
        )
        return jnp.maximum(top, jnp.max(s.reshape(CH // 8, 8, L), axis=0))

    def weigh(j, r, top, total, delta):
        for n in range(r, r + CH, 64):
            p = jnp.exp2((s_buf[j % 2, n : n + 64] - top) * EXP2)
            s_buf[j % 2, n : n + 64] = p
            e_ref[j, n : n + 64] = p.astype(BF)
            total += jnp.sum(p.reshape(8, 8, L), axis=0)
            delta += jnp.sum((p * p_buf[j % 2, n : n + 64]).reshape(8, 8, L), axis=0)
        return total, delta

    low = jnp.full((8, L), -jnp.inf, F32)
    zero = jnp.zeros((8, L), F32)
    ahead = low
    for r in range(0, MP, CH):
        ahead = multiply(0, r, ahead)
    for j in range(HD):
        top = jnp.max(ahead, axis=0, keepdims=True)
        total, delta, ahead = zero, zero, low
        for r in range(0, MP, CH):
            if j < HD - 1:
                ahead = multiply(j + 1, r, ahead)
            total, delta = weigh(j, r, top, total, delta)
        total = jnp.sum(total, axis=0, keepdims=True)
        delta = jnp.sum(delta, axis=0, keepdims=True)
        mean = delta / total
        for n in range(0, MP, 64):
            g_ref[j, n : n + 64] = (s_buf[j % 2, n : n + 64] * (p_buf[j % 2, n : n + 64] - mean)).astype(BF)
        st(j, top, total, delta)


def load_kernel(
    pos, x_hbm, wk_hbm, wv_hbm, q_hbm, c_hbm,
    x_ref, wk_ref, wv_ref, q_ref, c_ref, xs_ref, cs_ref,
    cb, sems,
):
    mine = pl.ds(pl.multiple_of(pos[0] * W, W), W)
    theirs = pl.ds(pl.multiple_of((1 - pos[0]) * W, W), W)
    pairs = [(x_hbm.at[pl.ds(n * CH, CH)], x_ref.at[pl.ds(n * CH, CH)]) for n in range(3)]
    pairs += [(c_hbm, cb), (wk_hbm.at[:, mine], wk_ref), (wv_hbm.at[:, mine], wv_ref), (q_hbm.at[:, mine], q_ref)]
    copies = [pltpu.make_async_copy(a, b, sems.at[n]) for n, (a, b) in enumerate(pairs)]
    for c in copies:
        c.start()
    for n in range(3):
        copies[n].wait()
        xs_ref[n * CH : n * CH + CH] = x_ref[n * CH : n * CH + CH].astype(F32)
    copies[3].wait()
    c_ref[...] = cb[:, mine]
    cs_ref[...] = cb[:, theirs].astype(F32)
    for c in copies[4:]:
        c.wait()


PROJ = pltpu.VMEM((2, MP, 256), BF)
MAPS = [pltpu.VMEM((HD, MP, L), BF), pltpu.VMEM((HD, MP, L), BF)]
BUFFERS = [pltpu.VMEM((2, MP, L), F32), pltpu.VMEM((2, MP, L), F32)]


def load(pos, x, wk, wv, q, c):
    return call(
        LOADL, 4, load_kernel, 1, [ANY] * 5, [VM] * 7,
        [
            pltpu.VMEM((MP, D), BF),
            pltpu.VMEM((D, W), BF),
            pltpu.VMEM((D, W), BF),
            pltpu.VMEM((L, W), BF),
            pltpu.VMEM((L, W), BF),
            pltpu.VMEM((MP, D), F32),
            pltpu.VMEM((L, W), F32),
        ],
        [pltpu.VMEM((L, D), BF), pltpu.SemaphoreType.DMA((7,))],
        pos, x, wk, wv, q, c,
    )


def home_kernel(pos, x_ref, wk_ref, wv_ref, q_ref, c_ref, k_ref, e_ref, g_ref, st_ref, v_buf, s_buf, p_buf):
    for h in range(2):
        for r in range(0, MP, CH):
            project(h, r, x_ref[r : r + CH], wk_ref, wv_ref, k_ref, v_buf)

    def st(j, *rows):
        for t, row in enumerate(rows):
            st_ref[t * HD + j : t * HD + j + 1] = row

    attend_heads(q_ref, c_ref, e_ref, g_ref, k_ref, v_buf, s_buf, p_buf, st)


def attend_home(pos, x, wk, wv, q, c):
    return call(
        HOME, 7, home_kernel, 1, [VM] * 5, [VM] * 4, [PROJ, *MAPS, pltpu.VMEM((3 * HD, L), F32)], [PROJ] + BUFFERS,
        pos, x, wk, wv, q, c,
    )


def away_kernel(
    pos, xs_ref, cs_ref, wk_ref, wv_ref, q_ref, st0_ref,
    x_ref, c_ref, k_ref, e_ref, g_ref, st_ref,
    v_buf, s_buf, p_buf,
):
    for n in range(0, MP, CH):
        x = xs_ref[n : n + CH].astype(BF)
        x_ref[n : n + CH] = x
        for h in range(2):
            project(h, n, x, wk_ref, wv_ref, k_ref, v_buf)
    c_ref[...] = cs_ref[...].astype(BF)

    def st(j, *rows):
        for t, row in enumerate(rows):
            st_ref[t * 8 + j : t * 8 + j + 1] = st0_ref[t * HD + j : t * HD + j + 1]
            st_ref[t * 8 + HD + j : t * 8 + HD + j + 1] = row

    attend_heads(q_ref, c_ref, e_ref, g_ref, k_ref, v_buf, s_buf, p_buf, st)


def attend_away(pos, x, c, wk, wv, q, st0):
    return call(
        AWAY, 7, away_kernel, 1, [VM] * 6, [VM] * 6,
        [pltpu.VMEM((MP, D), BF), pltpu.VMEM((L, W), BF), PROJ, *MAPS, pltpu.VMEM((24, L), F32)], [PROJ] + BUFFERS,
        pos, x, c, wk, wv, q, st0,
    )


def merge(parts):
    top = parts[0][:8]
    for p in parts[1:]:
        top = jnp.maximum(top, p[:8])
    total = delta = 0.0
    for p in parts:
        w = jnp.exp2((p[:8] - top) * EXP2)
        total += w * p[8:16]
        delta += w * p[16:24]
    return jnp.concatenate([top, total, delta], axis=0)


def place(core, mx, my, r1, r2):
    p1 = lax.rem(jnp.where(core == 0, mx, my) + r1, 4)
    p2 = lax.rem(jnp.where(core == 0, my, mx) + r2, 4)
    return jnp.where(core == 0, p1, p2), jnp.where(core == 0, p2, p1)


def weight_block(pos, r1, r2, x0_ref, x1_ref, d_ref, out):
    x, y = place(pos[0], pos[1], pos[2], r1, r2)
    rows = pl.ds(pl.multiple_of(((y % 2) * 4 + x) * 128, 128), 128)
    for t in range(2):
        cols = pl.ds(pl.multiple_of(t * W + y // 2 * 256, 256), 256)
        out[:, t * 256 : t * 256 + 256] = lax.dot_general(
            x0_ref[:, rows], d_ref[:MP, cols], TN, preferred_element_type=F32
        ) + lax.dot_general(x1_ref[:, rows], d_ref[MP:, cols], TN, preferred_element_type=F32)


def far_kernel(
    pos, st_ref, p0_ref, p1_ref, p2_ref, p3_ref, e0_ref, g0_ref, e1_ref, g1_ref, q_ref, c0_ref, c1_ref, x0_ref, x1_ref,
    fac_ref, d_ref, away_ref, ra_ref, rb_ref,
    right, left,
):
    local = st_ref[...]
    total = merge([p0_ref[...], p1_ref[...], p2_ref[...], p3_ref[...]])
    a = jnp.exp2((local[:8] - total[:8]) * EXP2) / total[8:16]
    eps = local[16:] / local[8:16] - total[16:] / total[8:16]
    fac = jnp.concatenate([a, eps], axis=0)
    fac_ref[...] = fac
    fac = fac.T
    for n, (e_ref, g_ref, c_ref) in enumerate(((e0_ref, g0_ref, c0_ref), (e1_ref, g1_ref, c1_ref))):
        for j in range(HD):
            cols = slice(j * HS, (j + 1) * HS)
            a = fac[:, n * HD + j : n * HD + j + 1]
            eps = fac[:, 8 + n * HD + j : 8 + n * HD + j + 1]
            aq = a * q_ref[:, cols].astype(F32)
            right[j % 2, :, :HS] = (eps * aq).astype(BF)
            right[j % 2, :, HS:] = (a * c_ref[:, cols].astype(F32)).astype(BF)
            left[j % 2] = aq.astype(BF)
            for r in range(0, MP, CH):
                both = jnp.dot(e_ref[j, r : r + CH], right[j % 2], preferred_element_type=F32)
                own = jnp.dot(g_ref[j, r : r + CH], left[j % 2], preferred_element_type=F32)
                rows = slice(n * MP + r, n * MP + r + CH)
                dk, dv = ((own + both[:, :HS]) * SCALE).astype(BF), both[:, HS:].astype(BF)
                for at, part in ((j * HS, dk), (W + j * HS, dv)):
                    d_ref[rows, at : at + HS] = part
                    if n == 1:
                        away_ref[r : r + CH, at : at + HS] = part.astype(F32)
    for n, (right, left) in enumerate((((2, 0), (2, 2)), ((2, 1), (2, 3)), ((1, 2), (3, 0)), ((1, 3), (3, 1)))):
        weight_block(pos, *right, x0_ref, x1_ref, d_ref, ra_ref.at[n])
        weight_block(pos, *left, x0_ref, x1_ref, d_ref, rb_ref.at[n])


def far_grads(pos, local, parts, e0, g0, e1, g1, q, c0, c1, x0, x1):
    half = pltpu.VMEM((4, 128, 512), F32)
    return call(
        14, 8, far_kernel, 1, [VM] + [whole((24, L))] * 4 + [VM] * 9, [VM] * 5,
        [pltpu.VMEM((16, L), F32), pltpu.VMEM((2 * MP, D), BF), pltpu.VMEM((MP, D), F32), half, half],
        [pltpu.VMEM((2, L, 2 * HS), BF), pltpu.VMEM((2, L, HS), BF)],
        pos, local, *parts, e0, g0, e1, g1, q, c0, c1, x0, x1,
    )


def near_kernel(
    pos, fac_ref, e0_ref, g0_ref, k0_ref, e1_ref, g1_ref, k1_ref, x0_ref, x1_ref, d_ref,
    r0_ref, r1_ref, r3_ref, l0_ref, l1_ref, l2_ref, l3_ref,
    lat,
):

    def block(n, _):
        weight_block(pos, 0, n, x0_ref, x1_ref, d_ref, r0_ref.at[n])
        weight_block(pos, 0, n + 2, x0_ref, x1_ref, d_ref, r0_ref.at[n + 2])
        weight_block(pos, 1, n, x0_ref, x1_ref, d_ref, r1_ref.at[n])
        weight_block(pos, 3, n + 2, x0_ref, x1_ref, d_ref, r3_ref.at[n])
        return 0

    lax.fori_loop(0, 2, block, 0)
    fac = fac_ref[...].T
    for n, (e_ref, g_ref, k_ref) in enumerate(((e0_ref, g0_ref, k0_ref), (e1_ref, g1_ref, k1_ref))):
        for j in range(HD):
            a = fac[:, n * HD + j : n * HD + j + 1]
            eps = fac[:, 8 + n * HD + j : 8 + n * HD + j + 1]
            k = k_ref[j // 2, :, j % 2 * HS : j % 2 * HS + HS]
            ek = lax.dot_general(e_ref[j], k, TN, preferred_element_type=F32)
            gk = lax.dot_general(g_ref[j], k, TN, preferred_element_type=F32)
            part = (a * SCALE) * (gk + eps * ek)
            at = slice(j % 2 * HS, j % 2 * HS + HS)
            if n == 0:
                lat[j // 2, :, at] = part
            else:
                lat[j // 2, :, at] += part
    core, mx, my = pos[0], pos[1], pos[2]
    for r1, out in enumerate((l0_ref, l1_ref, l2_ref, l3_ref)):
        for r2 in range(4):
            x, y = place(core, mx, my, r1, r2)
            for z in range(8):
                row = pl.multiple_of(((y % 2) * 4 + x) * 64 + z * 8, 8)
                out[r2, z // 2 * 8 : z // 2 * 8 + 8, z % 2 * 256 : z % 2 * 256 + 256] = lat[y // 2, pl.ds(row, 8)]


def near_grads(pos, fac, e0, g0, k0, e1, g1, k1, x0, x1, d):
    block, half, lat = (pltpu.VMEM(shape, F32) for shape in ((4, 128, 512), (2, 128, 512), (4, 32, 512)))
    return call(
        14, 8, near_kernel, 1, [VM] * 10, [VM] * 7, [block, half, half] + [lat] * 4, [pltpu.VMEM((2, L, 2 * HS), F32)],
        pos, fac, e0, g0, k0, e1, g1, k1, x0, x1, d,
    )


def input_kernel(pos, d_ref, wk_ref, wv_ref, got_ref, wk_hbm, wv_hbm, out_ref, wk_buf, wv_buf, total, sems):
    theirs = pl.ds(pl.multiple_of((1 - pos[0]) * W, W), W)
    copies = [
        pltpu.make_async_copy(a.at[:, theirs], b, sems.at[n])
        for n, (a, b) in enumerate(((wk_hbm, wk_buf), (wv_hbm, wv_buf)))
    ]
    for c in copies:
        c.start()
    for r in range(0, MP, CH):
        total[r : r + CH] = lax.dot_general(
            d_ref[r : r + CH, :W], wk_ref[...], NT, preferred_element_type=F32
        ) + lax.dot_general(d_ref[r : r + CH, W:], wv_ref[...], NT, preferred_element_type=F32)
    for c in copies:
        c.wait()
    for r in range(0, MP, CH):
        got = got_ref[r : r + CH].astype(BF)
        out_ref[r : r + CH] = (
            total[r : r + CH]
            + lax.dot_general(got[:, :W], wk_buf[...], NT, preferred_element_type=F32)
            + lax.dot_general(got[:, W:], wv_buf[...], NT, preferred_element_type=F32)
        ).astype(BF)


def input_grads(pos, d, wk, wv, got, key_weight, value_weight):
    return call(
        INPUT, 5.5, input_kernel, 1, [VM] * 4 + [ANY] * 2, [whole((MP, D))], [jax.ShapeDtypeStruct((MP, D), BF)],
        [pltpu.VMEM((D, W), BF), pltpu.VMEM((D, W), BF), pltpu.VMEM((MP, D), F32), pltpu.SemaphoreType.DMA((2,))],
        pos, d, wk, wv, got, key_weight, value_weight,
    )[0]


def fold_kernel(pos, r0_ref, l0_ref, right_ref, left_ref, ra_ref, rb_ref, far_ref, *outs):
    for n, out in enumerate(outs):
        rows = slice(128 * (n % 2), 128 * (n % 2) + 128)
        if n < 2:
            out[:128] = r0_ref[n] + right_ref[rows] + rb_ref[n + 2]
        else:
            out[:128] = r0_ref[n] + left_ref[rows] + ra_ref[n]
        lat = slice(256 + 32 * n, 288 + 32 * n)
        out[128:] = l0_ref[n] + far_ref[n] + right_ref[lat] + left_ref[lat]


def fold(pos, *args):
    return call(8, 0.5, fold_kernel, 1, [VM] * 7, [VM] * 4, [pltpu.VMEM((160, 512), F32)] * 4, [], pos, *args)


def turn_kernel(pos, a_ref, b_ref, c_ref, d_ref, *outs):
    outs[4][...] = a_ref[...] + b_ref[...] + c_ref[...] + d_ref[...]
    for r in range(8):
        z = lax.rem(pos[3] + r, 8)
        out = outs[r // 2]
        out[r % 2 * 16 : r % 2 * 16 + 16] = outs[4][pl.ds(pl.multiple_of(z * 16, 16), 16)]
        rows = outs[4][pl.ds(pl.multiple_of(128 + z // 2 * 8, 8), 8)]
        out[32:40, r % 2 * 256 : r % 2 * 256 + 256] = jnp.where(z % 2 == 0, rows[:, :256], rows[:, 256:])


def turn(pos, parts):
    return call(
        8, 0.7, turn_kernel, 1, [VM] * 4, [VM] * 4, [pltpu.VMEM((40, 512), F32)] * 4,
        [pltpu.VMEM((160, 512), F32)], pos, *parts,
    )


def body(queries, inputs, cotangent, key_weight, value_weight):
    seq, batch = lax.axis_index("seq"), lax.axis_index("batch")
    yl, mx, mz = seq // 32, seq // 8 % 4, seq % 8
    yh, core = batch // 2, batch % 2
    pos = jnp.stack([core, mx, yh * 2 + yl, mz]).astype(jnp.int32)

    over = lambda y, x, z, c: (y, x, z, c + 1)
    x0, wk, wv, q, c0, xs, cs = load(pos, inputs[0], key_weight, value_weight, queries, cotangent[0])
    xs, cs = send(xs, over), send(cs, over)
    k0, e0, g0, st0 = attend_home(pos, x0, wk, wv, q, c0)
    x1, c1, k1, e1, g1, local = attend_away(pos, xs, cs, wk, wv, q, st0)

    stats = local
    stats = merge([stats] + [send(stats, lambda y, x, z, c, n=n: (y, x + n, z, c)) for n in (1, 2, 3)])
    stats = merge([stats] + [send(stats, lambda y, x, z, c, n=n: (y, x, z + n, c)) for n in (2, 4, 6)])
    parts = [stats] + [
        send(stats, lambda y, x, z, c, n=n: (y ^ (n & 1), x, z + (n >> 1), c)) for n in (1, 2, 3)
    ]

    fac, d, back, ra, rb = far_grads(pos, local, parts, e0, g0, e1, g1, q, c0, c1, x0, x1)

    def first(n):
        return lambda y, x, z, c: (y, x + n, z, c) if c == 0 else (y + n, x, z, c)

    def second(n):
        return lambda y, x, z, c: (y + n, x, z, c) if c == 0 else (y, x + n, z, c)

    ra, rb = send(ra, first(1)), send(rb, first(-1))
    r0, r1, r3, l0, l1, l2, l3 = near_grads(pos, fac, e0, g0, k0, e1, g1, k1, x0, x1, d)
    back = send(back, over)
    right = jnp.concatenate([(r1 + ra[:2]).reshape(256, 512), l1.reshape(128, 512)], axis=0)
    left = jnp.concatenate([(r3 + rb[:2]).reshape(256, 512), l3.reshape(128, 512)], axis=0)
    d, right_buf, left_buf = lax.optimization_barrier((d, right, left))
    right, left, far_l = send(right, first(1)), send(left, first(-1)), send(l2, first(2))
    grad_in = input_grads(pos, d, wk, wv, back, key_weight, value_weight)
    r0, grad_in = lax.optimization_barrier((r0, grad_in))
    parts = fold(pos, r0, l0, right, left, ra, rb, far_l)
    parts = turn(pos, [parts[0]] + [send(parts[n], second(n)) for n in (2, 1, 3)])
    parts = [parts[0]] + [send(parts[n], lambda y, x, z, c, n=n: (y, x, z + 2 * n, c)) for n in (2, 1, 3)]
    total = parts[0] + parts[1] + parts[2] + parts[3]
    here = jnp.concatenate([total[:16], jnp.concatenate([total[32:, :256], jnp.zeros((8, 256), F32)], 0)], axis=1)
    next_z = jnp.concatenate([total[16:32], jnp.concatenate([total[32:, 256:], jnp.zeros((8, 256), F32)], 0)], axis=1)
    near = here + send(next_z, lambda y, x, z, c: (y, x, z + 1, c))
    far = send(here, lambda y, x, z, c: (y + 2, x, z, c)) + send(next_z, lambda y, x, z, c: (y + 2, x, z + 1, c))
    pair = jnp.where(yh == 0, jnp.concatenate([near, far], axis=1), jnp.concatenate([far, near], axis=1))
    other = send(pair, over)
    low, high = jnp.where(core == 0, pair, other), jnp.where(core == 0, other, pair)

    def pick(start, stop, rows):
        return jnp.concatenate([a[:rows, b + start : b + stop] for a in (low, high) for b in (0, 768)], axis=1)

    return grad_in[None], pick(512, 768, 8), pick(0, 256, 16), pick(256, 512, 16)


def solution(mesh):
    placed = (P(), P("batch", "seq", None), P("batch", None, None), P(), P())
    return jax.shard_map(
        body,
        mesh=mesh,
        in_specs=placed,
        out_specs=(P("batch", "seq", None), P("seq", None), P("seq", None), P("seq", None)),
        check_vma=False,
    )
```

```python
import math

import jax
import jax.numpy as jnp
from jax import lax
from jax.experimental import pallas as pl
from jax.experimental.pallas import tpu as pltpu
from jax.sharding import PartitionSpec as P

L = 512
D = 1024
HS = 128
HD = 4
W = HD * HS
MP = 768
CH = 256
SCALE = 1.0 / math.sqrt(128.0)
EXP2 = SCALE * math.log2(math.e)
BF = jnp.bfloat16
F32 = jnp.float32
AXES = ("seq", "batch")
NT = (((1,), (1,)), ((), ()))
TN = (((0,), (0,)), ((), ()))
VM = pl.BlockSpec(memory_space=pltpu.VMEM)
ANY = pl.BlockSpec(memory_space=pl.ANY)
HOME = 12
LOADL = 52
AWAY = 12
INPUT = 24


def routes(move):
    pairs = []
    for seq in range(64):
        for batch in range(4):
            yl, x, z = seq // 32, seq // 8 % 4, seq % 8
            yh, c = batch // 2, batch % 2
            y, x, z, c = move(yh * 2 + yl, x, z, c)
            y, x, z, c = y % 4, x % 4, z % 8, c % 2
            pairs.append((seq * 4 + batch, (((y % 2) * 4 + x) * 8 + z) * 4 + (y // 2) * 2 + c))
    return pairs


def send(value, move):
    return lax.ppermute(value, AXES, routes(move))


def whole(shape):
    return pl.BlockSpec(shape, lambda i, *_: (0,) * len(shape))


def call(limit, us, kernel, grid, in_specs, out_specs, out_shape, scratch, *args):
    return pl.pallas_call(
        kernel,
        grid_spec=pltpu.PrefetchScalarGridSpec(
            num_scalar_prefetch=1, grid=(grid,), in_specs=in_specs, out_specs=out_specs, scratch_shapes=scratch
        ),
        out_shape=out_shape,
        compiler_params=pltpu.CompilerParams(vmem_limit_bytes=limit * 2**20),
        cost_estimate=pl.CostEstimate(flops=1, bytes_accessed=int(us * 3.6e6), transcendentals=0),
    )(*args)


def project(h, r, x, wk_ref, wv_ref, k_buf, v_buf):
    cols = slice(h * 256, h * 256 + 256)
    k_buf[h, r : r + CH] = jnp.dot(x, wk_ref[:, cols], preferred_element_type=F32).astype(BF)
    v_buf[h, r : r + CH] = jnp.dot(x, wv_ref[:, cols], preferred_element_type=F32).astype(BF)


def attend_heads(q_ref, c_ref, e_ref, g_ref, k_buf, v_buf, s_buf, p_buf, st):
    def multiply(j, r, top):
        h, cols, mine = j // 2, slice(j % 2 * HS, j % 2 * HS + HS), slice(j * HS, j * HS + HS)
        s = lax.dot_general(k_buf[h, r : r + CH, cols], q_ref[:, mine], NT, preferred_element_type=F32)
        s_buf[j % 2, r : r + CH] = s
        p_buf[j % 2, r : r + CH] = lax.dot_general(
            v_buf[h, r : r + CH, cols], c_ref[:, mine], NT, preferred_element_type=F32
        )
        return jnp.maximum(top, jnp.max(s.reshape(CH // 8, 8, L), axis=0))

    def weigh(j, r, top, total, delta):
        for n in range(r, r + CH, 64):
            p = jnp.exp2((s_buf[j % 2, n : n + 64] - top) * EXP2)
            s_buf[j % 2, n : n + 64] = p
            e_ref[j, n : n + 64] = p.astype(BF)
            total += jnp.sum(p.reshape(8, 8, L), axis=0)
            delta += jnp.sum((p * p_buf[j % 2, n : n + 64]).reshape(8, 8, L), axis=0)
        return total, delta

    low = jnp.full((8, L), -jnp.inf, F32)
    zero = jnp.zeros((8, L), F32)
    ahead = low
    for r in range(0, MP, CH):
        ahead = multiply(0, r, ahead)
    for j in range(HD):
        top = jnp.max(ahead, axis=0, keepdims=True)
        total, delta, ahead = zero, zero, low
        for r in range(0, MP, CH):
            if j < HD - 1:
                ahead = multiply(j + 1, r, ahead)
            total, delta = weigh(j, r, top, total, delta)
        total = jnp.sum(total, axis=0, keepdims=True)
        delta = jnp.sum(delta, axis=0, keepdims=True)
        mean = delta / total
        for n in range(0, MP, 64):
            g_ref[j, n : n + 64] = (s_buf[j % 2, n : n + 64] * (p_buf[j % 2, n : n + 64] - mean)).astype(BF)
        st(j, top, total, delta)


def load_kernel(
    x_hbm, wk_hbm, wv_hbm, q_hbm, c_hbm,
    x_ref, wk_ref, wv_ref, q_ref, c_ref, xs_ref, cs_ref,
    cb, sems,
):
    core = lax.rem(lax.axis_index("batch"), 2)
    mine = pl.ds(pl.multiple_of(core * W, W), W)
    theirs = pl.ds(pl.multiple_of((1 - core) * W, W), W)
    pairs = [(x_hbm.at[pl.ds(n * CH, CH)], x_ref.at[pl.ds(n * CH, CH)]) for n in range(3)]
    pairs += [(c_hbm, cb), (wk_hbm.at[:, mine], wk_ref), (wv_hbm.at[:, mine], wv_ref), (q_hbm.at[:, mine], q_ref)]
    copies = [pltpu.make_async_copy(a, b, sems.at[n]) for n, (a, b) in enumerate(pairs)]
    for c in copies:
        c.start()
    for n in range(3):
        copies[n].wait()
        xs_ref[n * CH : n * CH + CH] = x_ref[n * CH : n * CH + CH].astype(F32)
    copies[3].wait()
    c_ref[...] = cb[:, mine]
    cs_ref[...] = cb[:, theirs].astype(F32)
    for c in copies[4:]:
        c.wait()


PROJ = pltpu.VMEM((2, MP, 256), BF)
MAPS = [pltpu.VMEM((HD, MP, L), BF), pltpu.VMEM((HD, MP, L), BF)]
BUFFERS = [pltpu.VMEM((2, MP, L), F32), pltpu.VMEM((2, MP, L), F32)]


def load(x, wk, wv, q, c):
    return pl.pallas_call(
        load_kernel,
        in_specs=[ANY] * 5,
        out_specs=[VM] * 7,
        out_shape=[
            pltpu.VMEM((MP, D), BF),
            pltpu.VMEM((D, W), BF),
            pltpu.VMEM((D, W), BF),
            pltpu.VMEM((L, W), BF),
            pltpu.VMEM((L, W), BF),
            pltpu.VMEM((MP, D), F32),
            pltpu.VMEM((L, W), F32),
        ],
        scratch_shapes=[pltpu.VMEM((L, D), BF), pltpu.SemaphoreType.DMA((7,))],
        compiler_params=pltpu.CompilerParams(vmem_limit_bytes=LOADL * 2**20),
        cost_estimate=pl.CostEstimate(flops=1, bytes_accessed=14 * 10**6, transcendentals=0),
    )(x, wk, wv, q, c)


def home_kernel(pos, x_ref, wk_ref, wv_ref, q_ref, c_ref, k_ref, e_ref, g_ref, st_ref, v_buf, s_buf, p_buf):
    for h in range(2):
        for r in range(0, MP, CH):
            project(h, r, x_ref[r : r + CH], wk_ref, wv_ref, k_ref, v_buf)

    def st(j, *rows):
        for t, row in enumerate(rows):
            st_ref[t * HD + j : t * HD + j + 1] = row

    attend_heads(q_ref, c_ref, e_ref, g_ref, k_ref, v_buf, s_buf, p_buf, st)


def attend_home(pos, x, wk, wv, q, c):
    return call(
        HOME, 7, home_kernel, 1, [VM] * 5, [VM] * 4, [PROJ, *MAPS, pltpu.VMEM((3 * HD, L), F32)], [PROJ] + BUFFERS,
        pos, x, wk, wv, q, c,
    )


def away_kernel(
    pos, xs_ref, cs_ref, wk_ref, wv_ref, q_ref, st0_ref,
    x_ref, c_ref, k_ref, e_ref, g_ref, st_ref,
    v_buf, s_buf, p_buf,
):
    for n in range(0, MP, CH):
        x = xs_ref[n : n + CH].astype(BF)
        x_ref[n : n + CH] = x
        for h in range(2):
            project(h, n, x, wk_ref, wv_ref, k_ref, v_buf)
    c_ref[...] = cs_ref[...].astype(BF)

    def st(j, *rows):
        for t, row in enumerate(rows):
            st_ref[t * 8 + j : t * 8 + j + 1] = st0_ref[t * HD + j : t * HD + j + 1]
            st_ref[t * 8 + HD + j : t * 8 + HD + j + 1] = row

    attend_heads(q_ref, c_ref, e_ref, g_ref, k_ref, v_buf, s_buf, p_buf, st)


def attend_away(pos, x, c, wk, wv, q, st0):
    return call(
        AWAY, 7, away_kernel, 1, [VM] * 6, [VM] * 6,
        [pltpu.VMEM((MP, D), BF), pltpu.VMEM((L, W), BF), PROJ, *MAPS, pltpu.VMEM((24, L), F32)], [PROJ] + BUFFERS,
        pos, x, c, wk, wv, q, st0,
    )


def merge(parts):
    top = parts[0][:8]
    for p in parts[1:]:
        top = jnp.maximum(top, p[:8])
    total = delta = 0.0
    for p in parts:
        w = jnp.exp2((p[:8] - top) * EXP2)
        total += w * p[8:16]
        delta += w * p[16:24]
    return jnp.concatenate([top, total, delta], axis=0)


def place(core, mx, my, r1, r2):
    p1 = lax.rem(jnp.where(core == 1, mx, my) + r1, 4)
    p2 = lax.rem(jnp.where(core == 1, my, mx) + r2, 4)
    return jnp.where(core == 1, p1, p2), jnp.where(core == 1, p2, p1)


def weight_block(pos, r1, r2, x0_ref, x1_ref, d_ref, out):
    x, y = place(pos[0], pos[1], pos[2], r1, r2)
    rows = pl.ds(pl.multiple_of(((y % 2) * 4 + x) * 128, 128), 128)
    x0, x1 = x0_ref[:, rows].T, x1_ref[:, rows].T
    for t in range(2):
        cols = pl.ds(pl.multiple_of(t * W + y // 2 * 256, 256), 256)
        out[:, t * 256 : t * 256 + 256] = jnp.dot(x0, d_ref[:MP, cols], preferred_element_type=F32) + jnp.dot(
            x1, d_ref[MP:, cols], preferred_element_type=F32
        )


def far_kernel(
    pos, st_ref, p0_ref, p1_ref, p2_ref, p3_ref, e0_ref, g0_ref, e1_ref, g1_ref, q_ref, c0_ref, c1_ref, x0_ref, x1_ref,
    fac_ref, d_ref, away_ref, ra_ref, rb_ref,
    right, left,
):
    local = st_ref[...]
    total = merge([p0_ref[...], p1_ref[...], p2_ref[...], p3_ref[...]])
    a = jnp.exp2((local[:8] - total[:8]) * EXP2) / total[8:16]
    eps = local[16:] / local[8:16] - total[16:] / total[8:16]
    fac = jnp.concatenate([a, eps], axis=0)
    fac_ref[...] = fac
    fac = fac.T
    for n, (e_ref, g_ref, c_ref) in enumerate(((e0_ref, g0_ref, c0_ref), (e1_ref, g1_ref, c1_ref))):
        for j in range(HD):
            cols = slice(j * HS, (j + 1) * HS)
            a = fac[:, n * HD + j : n * HD + j + 1]
            eps = fac[:, 8 + n * HD + j : 8 + n * HD + j + 1]
            aq = a * q_ref[:, cols].astype(F32)
            right[j % 2, :, :HS] = (eps * aq).astype(BF)
            right[j % 2, :, HS:] = (a * c_ref[:, cols].astype(F32)).astype(BF)
            left[j % 2] = aq.astype(BF)
            for r in range(0, MP, CH):
                both = jnp.dot(e_ref[j, r : r + CH], right[j % 2], preferred_element_type=F32)
                own = jnp.dot(g_ref[j, r : r + CH], left[j % 2], preferred_element_type=F32)
                rows = slice(n * MP + r, n * MP + r + CH)
                dk, dv = ((own + both[:, :HS]) * SCALE).astype(BF), both[:, HS:].astype(BF)
                for at, part in ((j * HS, dk), (W + j * HS, dv)):
                    d_ref[rows, at : at + HS] = part
                    if n == 1:
                        away_ref[r : r + CH, at : at + HS] = part.astype(F32)
    for n, (right, left) in enumerate((((2, 0), (2, 2)), ((2, 1), (2, 3)), ((1, 2), (3, 0)), ((1, 3), (3, 1)))):
        weight_block(pos, *right, x0_ref, x1_ref, d_ref, ra_ref.at[n])
        weight_block(pos, *left, x0_ref, x1_ref, d_ref, rb_ref.at[n])


def far_grads(pos, local, parts, e0, g0, e1, g1, q, c0, c1, x0, x1):
    half = pltpu.VMEM((4, 128, 512), F32)
    return call(
        14, 8, far_kernel, 1, [VM] + [whole((24, L))] * 4 + [VM] * 9, [VM] * 5,
        [pltpu.VMEM((16, L), F32), pltpu.VMEM((2 * MP, D), BF), pltpu.VMEM((MP, D), F32), half, half],
        [pltpu.VMEM((2, L, 2 * HS), BF), pltpu.VMEM((2, L, HS), BF)],
        pos, local, *parts, e0, g0, e1, g1, q, c0, c1, x0, x1,
    )


def near_kernel(
    pos, fac_ref, e0_ref, g0_ref, k0_ref, e1_ref, g1_ref, k1_ref, x0_ref, x1_ref, d_ref,
    r0_ref, r1_ref, r3_ref, l0_ref, l1_ref, l2_ref, l3_ref,
    lat,
):

    def block(n, _):
        weight_block(pos, 0, n, x0_ref, x1_ref, d_ref, r0_ref.at[n])
        weight_block(pos, 0, n + 2, x0_ref, x1_ref, d_ref, r0_ref.at[n + 2])
        weight_block(pos, 1, n, x0_ref, x1_ref, d_ref, r1_ref.at[n])
        weight_block(pos, 3, n + 2, x0_ref, x1_ref, d_ref, r3_ref.at[n])
        return 0

    lax.fori_loop(0, 2, block, 0)
    fac = fac_ref[...].T
    for n, (e_ref, g_ref, k_ref) in enumerate(((e0_ref, g0_ref, k0_ref), (e1_ref, g1_ref, k1_ref))):
        for j in range(HD):
            a = fac[:, n * HD + j : n * HD + j + 1]
            eps = fac[:, 8 + n * HD + j : 8 + n * HD + j + 1]
            k = k_ref[j // 2, :, j % 2 * HS : j % 2 * HS + HS]
            ek = lax.dot_general(e_ref[j], k, TN, preferred_element_type=F32)
            gk = lax.dot_general(g_ref[j], k, TN, preferred_element_type=F32)
            part = (a * SCALE) * (gk + eps * ek)
            at = slice(j % 2 * HS, j % 2 * HS + HS)
            if n == 0:
                lat[j // 2, :, at] = part
            else:
                lat[j // 2, :, at] += part
    core, mx, my = pos[0], pos[1], pos[2]
    for r1, out in enumerate((l0_ref, l1_ref, l2_ref, l3_ref)):
        for r2 in range(4):
            x, y = place(core, mx, my, r1, r2)
            for z in range(8):
                row = pl.multiple_of(((y % 2) * 4 + x) * 64 + z * 8, 8)
                out[r2, z // 2 * 8 : z // 2 * 8 + 8, z % 2 * 256 : z % 2 * 256 + 256] = lat[y // 2, pl.ds(row, 8)]


def near_grads(pos, fac, e0, g0, k0, e1, g1, k1, x0, x1, d):
    block, half, lat = (pltpu.VMEM(shape, F32) for shape in ((4, 128, 512), (2, 128, 512), (4, 32, 512)))
    return call(
        14, 8, near_kernel, 1, [VM] * 10, [VM] * 7, [block, half, half] + [lat] * 4, [pltpu.VMEM((2, L, 2 * HS), F32)],
        pos, fac, e0, g0, k0, e1, g1, k1, x0, x1, d,
    )


def input_kernel(pos, d_ref, wk_ref, wv_ref, got_ref, wk_hbm, wv_hbm, out_ref, wk_buf, wv_buf, total, sems):
    theirs = pl.ds(pl.multiple_of((1 - pos[0]) * W, W), W)
    copies = [
        pltpu.make_async_copy(a.at[:, theirs], b, sems.at[n])
        for n, (a, b) in enumerate(((wk_hbm, wk_buf), (wv_hbm, wv_buf)))
    ]
    for c in copies:
        c.start()
    for r in range(0, MP, CH):
        total[r : r + CH] = lax.dot_general(
            d_ref[r : r + CH, :W], wk_ref[...], NT, preferred_element_type=F32
        ) + lax.dot_general(d_ref[r : r + CH, W:], wv_ref[...], NT, preferred_element_type=F32)
    for c in copies:
        c.wait()
    for r in range(0, MP, CH):
        got = got_ref[r : r + CH].astype(BF)
        out_ref[r : r + CH] = (
            total[r : r + CH]
            + lax.dot_general(got[:, :W], wk_buf[...], NT, preferred_element_type=F32)
            + lax.dot_general(got[:, W:], wv_buf[...], NT, preferred_element_type=F32)
        ).astype(BF)


def input_grads(pos, d, wk, wv, got, key_weight, value_weight):
    return call(
        INPUT, 5.5, input_kernel, 1, [VM] * 4 + [ANY] * 2, [whole((MP, D))], [jax.ShapeDtypeStruct((MP, D), BF)],
        [pltpu.VMEM((D, W), BF), pltpu.VMEM((D, W), BF), pltpu.VMEM((MP, D), F32), pltpu.SemaphoreType.DMA((2,))],
        pos, d, wk, wv, got, key_weight, value_weight,
    )[0]


def fold_kernel(pos, r0_ref, l0_ref, right_ref, left_ref, ra_ref, rb_ref, far_ref, *outs):
    for n, out in enumerate(outs):
        rows = slice(128 * (n % 2), 128 * (n % 2) + 128)
        if n < 2:
            out[:128] = r0_ref[n] + right_ref[rows] + rb_ref[n + 2]
        else:
            out[:128] = r0_ref[n] + left_ref[rows] + ra_ref[n]
        lat = slice(256 + 32 * n, 288 + 32 * n)
        out[128:] = l0_ref[n] + far_ref[n] + right_ref[lat] + left_ref[lat]


def fold(pos, *args):
    return call(8, 0.5, fold_kernel, 1, [VM] * 7, [VM] * 4, [pltpu.VMEM((160, 512), F32)] * 4, [], pos, *args)


def turn_kernel(pos, a_ref, b_ref, c_ref, d_ref, *outs):
    outs[4][...] = a_ref[...] + b_ref[...] + c_ref[...] + d_ref[...]
    for r in range(8):
        z = lax.rem(pos[3] + r, 8)
        out = outs[r // 2]
        out[r % 2 * 16 : r % 2 * 16 + 16] = outs[4][pl.ds(pl.multiple_of(z * 16, 16), 16)]
        rows = outs[4][pl.ds(pl.multiple_of(128 + z // 2 * 8, 8), 8)]
        out[32:40, r % 2 * 256 : r % 2 * 256 + 256] = jnp.where(z % 2 == 0, rows[:, :256], rows[:, 256:])


def turn(pos, parts):
    return call(
        8, 0.7, turn_kernel, 1, [VM] * 4, [VM] * 4, [pltpu.VMEM((40, 512), F32)] * 4,
        [pltpu.VMEM((160, 512), F32)], pos, *parts,
    )


def body(queries, inputs, cotangent, key_weight, value_weight):
    seq, batch = lax.axis_index("seq"), lax.axis_index("batch")
    yl, mx, mz = seq // 32, seq // 8 % 4, seq % 8
    yh, core = batch // 2, batch % 2
    pos = jnp.stack([core, mx, yh * 2 + yl, mz]).astype(jnp.int32)

    over = lambda y, x, z, c: (y, x, z, c + 1)
    x0, wk, wv, q, c0, xs, cs = load(inputs[0], key_weight, value_weight, queries, cotangent[0])
    xs, cs = send(xs, over), send(cs, over)
    k0, e0, g0, st0 = attend_home(pos, x0, wk, wv, q, c0)
    x1, c1, k1, e1, g1, local = attend_away(pos, xs, cs, wk, wv, q, st0)

    stats = local
    stats = merge([stats] + [send(stats, lambda y, x, z, c, n=n: (y, x + n, z, c)) for n in (1, 2, 3)])
    stats = merge([stats] + [send(stats, lambda y, x, z, c, n=n: (y, x, z + n, c)) for n in (2, 4, 6)])
    parts = [stats] + [
        send(stats, lambda y, x, z, c, n=n: (y ^ (n & 1), x, z + (n >> 1), c)) for n in (1, 2, 3)
    ]

    fac, d, back, ra, rb = far_grads(pos, local, parts, e0, g0, e1, g1, q, c0, c1, x0, x1)

    def first(n):
        return lambda y, x, z, c: (y, x + n, z, c) if c == 1 else (y + n, x, z, c)

    def second(n):
        return lambda y, x, z, c: (y + n, x, z, c) if c == 1 else (y, x + n, z, c)

    ra, rb = send(ra, first(1)), send(rb, first(-1))
    r0, r1, r3, l0, l1, l2, l3 = near_grads(pos, fac, e0, g0, k0, e1, g1, k1, x0, x1, d)
    back = send(back, over)
    right = jnp.concatenate([(r1 + ra[:2]).reshape(256, 512), l1.reshape(128, 512)], axis=0)
    left = jnp.concatenate([(r3 + rb[:2]).reshape(256, 512), l3.reshape(128, 512)], axis=0)
    d, right_buf, left_buf = lax.optimization_barrier((d, right, left))
    right, left, far_l = send(right, first(1)), send(left, first(-1)), send(l2, first(2))
    grad_in = input_grads(pos, d, wk, wv, back, key_weight, value_weight)
    r0, grad_in = lax.optimization_barrier((r0, grad_in))
    parts = fold(pos, r0, l0, right, left, ra, rb, far_l)
    parts = turn(pos, [parts[0]] + [send(parts[n], second(n)) for n in (2, 1, 3)])
    parts = [parts[0]] + [send(parts[n], lambda y, x, z, c, n=n: (y, x, z + 2 * n, c)) for n in (2, 1, 3)]
    total = parts[0] + parts[1] + parts[2] + parts[3]
    here = jnp.concatenate([total[:16], jnp.concatenate([total[32:, :256], jnp.zeros((8, 256), F32)], 0)], axis=1)
    next_z = jnp.concatenate([total[16:32], jnp.concatenate([total[32:, 256:], jnp.zeros((8, 256), F32)], 0)], axis=1)
    near = here + send(next_z, lambda y, x, z, c: (y, x, z + 1, c))
    far = send(here, lambda y, x, z, c: (y + 2, x, z, c)) + send(next_z, lambda y, x, z, c: (y + 2, x, z + 1, c))
    pair = jnp.where(yh == 0, jnp.concatenate([near, far], axis=1), jnp.concatenate([far, near], axis=1))
    other = send(pair, over)
    low, high = jnp.where(core == 0, pair, other), jnp.where(core == 0, other, pair)

    def pick(start, stop, rows):
        return jnp.concatenate([a[:rows, b + start : b + stop] for a in (low, high) for b in (0, 768)], axis=1)

    return grad_in[None], pick(512, 768, 8), pick(0, 256, 16), pick(256, 512, 16)


def solution(mesh):
    placed = (P(), P("batch", "seq", None), P("batch", None, None), P(), P())
    return jax.shard_map(
        body,
        mesh=mesh,
        in_specs=placed,
        out_specs=(P("batch", "seq", None), P("seq", None), P("seq", None), P("seq", None)),
        check_vma=False,
    )
```

```python
import math

import jax
import jax.numpy as jnp
from jax import lax
from jax.experimental import pallas as pl
from jax.experimental.pallas import tpu as pltpu
from jax.sharding import PartitionSpec as P

L = 512
D = 1024
HS = 128
HD = 4
W = HD * HS
MP = 768
CH = 256
SCALE = 1.0 / math.sqrt(128.0)
EXP2 = SCALE * math.log2(math.e)
BF = jnp.bfloat16
F32 = jnp.float32
AXES = ("seq", "batch")
NT = (((1,), (1,)), ((), ()))
TN = (((0,), (0,)), ((), ()))
VM = pl.BlockSpec(memory_space=pltpu.VMEM)
ANY = pl.BlockSpec(memory_space=pl.ANY)
HOME = 12
LOADL = 52
AWAY = 12
INPUT = 24


def routes(move):
    pairs = []
    for seq in range(64):
        for batch in range(4):
            yl, x, z = seq // 32, seq // 8 % 4, seq % 8
            yh, c = batch // 2, batch % 2
            y, x, z, c = move(yh * 2 + yl, x, z, c)
            y, x, z, c = y % 4, x % 4, z % 8, c % 2
            pairs.append((seq * 4 + batch, (((y % 2) * 4 + x) * 8 + z) * 4 + (y // 2) * 2 + c))
    return pairs


def send(value, move):
    return lax.ppermute(value, AXES, routes(move))


def whole(shape):
    return pl.BlockSpec(shape, lambda i, *_: (0,) * len(shape))


def call(limit, us, kernel, grid, in_specs, out_specs, out_shape, scratch, *args):
    return pl.pallas_call(
        kernel,
        grid_spec=pltpu.PrefetchScalarGridSpec(
            num_scalar_prefetch=1, grid=(grid,), in_specs=in_specs, out_specs=out_specs, scratch_shapes=scratch
        ),
        out_shape=out_shape,
        compiler_params=pltpu.CompilerParams(vmem_limit_bytes=limit * 2**20),
        cost_estimate=pl.CostEstimate(flops=1, bytes_accessed=int(us * 3.6e6), transcendentals=0),
    )(*args)


def project(h, r, x, wk_ref, wv_ref, k_buf, v_buf):
    cols = slice(h * 256, h * 256 + 256)
    k_buf[h, r : r + CH] = jnp.dot(x, wk_ref[:, cols], preferred_element_type=F32).astype(BF)
    v_buf[h, r : r + CH] = jnp.dot(x, wv_ref[:, cols], preferred_element_type=F32).astype(BF)


def attend_heads(q_ref, c_ref, e_ref, g_ref, k_buf, v_buf, s_buf, p_buf, st):
    def multiply(j, r, top):
        h, cols, mine = j // 2, slice(j % 2 * HS, j % 2 * HS + HS), slice(j * HS, j * HS + HS)
        s = lax.dot_general(k_buf[h, r : r + CH, cols], q_ref[:, mine], NT, preferred_element_type=F32)
        s_buf[j % 2, r : r + CH] = s
        p_buf[j % 2, r : r + CH] = lax.dot_general(
            v_buf[h, r : r + CH, cols], c_ref[:, mine], NT, preferred_element_type=F32
        )
        return jnp.maximum(top, jnp.max(s.reshape(CH // 8, 8, L), axis=0))

    def weigh(j, r, top, total, delta):
        for n in range(r, r + CH, 64):
            p = jnp.exp2((s_buf[j % 2, n : n + 64] - top) * EXP2)
            s_buf[j % 2, n : n + 64] = p
            e_ref[j, n : n + 64] = p.astype(BF)
            total += jnp.sum(p.reshape(8, 8, L), axis=0)
            delta += jnp.sum((p * p_buf[j % 2, n : n + 64]).reshape(8, 8, L), axis=0)
        return total, delta

    low = jnp.full((8, L), -jnp.inf, F32)
    zero = jnp.zeros((8, L), F32)
    ahead = low
    for r in range(0, MP, CH):
        ahead = multiply(0, r, ahead)
    for j in range(HD):
        top = jnp.max(ahead, axis=0, keepdims=True)
        total, delta, ahead = zero, zero, low
        for r in range(0, MP, CH):
            if j < HD - 1:
                ahead = multiply(j + 1, r, ahead)
            total, delta = weigh(j, r, top, total, delta)
        total = jnp.sum(total, axis=0, keepdims=True)
        delta = jnp.sum(delta, axis=0, keepdims=True)
        mean = delta / total
        for n in range(0, MP, 64):
            g_ref[j, n : n + 64] = (s_buf[j % 2, n : n + 64] * (p_buf[j % 2, n : n + 64] - mean)).astype(BF)
        st(j, top, total, delta)


def load_kernel(
    pos, x_hbm, wk_hbm, wv_hbm, q_hbm, c_hbm,
    x_ref, wk_ref, wv_ref, q_ref, c_ref, xs_ref, cs_ref,
    cb, sems,
):
    mine = pl.ds(pl.multiple_of(pos[0] * W, W), W)
    theirs = pl.ds(pl.multiple_of((1 - pos[0]) * W, W), W)
    pairs = [(x_hbm.at[pl.ds(n * CH, CH)], x_ref.at[pl.ds(n * CH, CH)]) for n in range(3)]
    pairs += [(c_hbm, cb), (wk_hbm.at[:, mine], wk_ref), (wv_hbm.at[:, mine], wv_ref), (q_hbm.at[:, mine], q_ref)]
    copies = [pltpu.make_async_copy(a, b, sems.at[n]) for n, (a, b) in enumerate(pairs)]
    for c in copies:
        c.start()
    for n in range(3):
        copies[n].wait()
        xs_ref[n * CH : n * CH + CH] = x_ref[n * CH : n * CH + CH].astype(F32)
    copies[3].wait()
    c_ref[...] = cb[:, mine]
    cs_ref[...] = cb[:, theirs].astype(F32)
    for c in copies[4:]:
        c.wait()


PROJ = pltpu.VMEM((2, MP, 256), BF)
MAPS = [pltpu.VMEM((HD, MP, L), BF), pltpu.VMEM((HD, MP, L), BF)]
BUFFERS = [pltpu.VMEM((2, MP, L), F32), pltpu.VMEM((2, MP, L), F32)]


def load(pos, x, wk, wv, q, c):
    return call(
        LOADL, 4, load_kernel, 1, [ANY] * 5, [VM] * 7,
        [
            pltpu.VMEM((MP, D), BF),
            pltpu.VMEM((D, W), BF),
            pltpu.VMEM((D, W), BF),
            pltpu.VMEM((L, W), BF),
            pltpu.VMEM((L, W), BF),
            pltpu.VMEM((MP, D), F32),
            pltpu.VMEM((L, W), F32),
        ],
        [pltpu.VMEM((L, D), BF), pltpu.SemaphoreType.DMA((7,))],
        pos, x, wk, wv, q, c,
    )


def home_kernel(pos, x_ref, wk_ref, wv_ref, q_ref, c_ref, k_ref, e_ref, g_ref, st_ref, v_buf, s_buf, p_buf):
    for h in range(2):
        for r in range(0, MP, CH):
            project(h, r, x_ref[r : r + CH], wk_ref, wv_ref, k_ref, v_buf)

    def st(j, *rows):
        for t, row in enumerate(rows):
            st_ref[t * HD + j : t * HD + j + 1] = row

    attend_heads(q_ref, c_ref, e_ref, g_ref, k_ref, v_buf, s_buf, p_buf, st)


def attend_home(pos, x, wk, wv, q, c):
    return call(
        HOME, 7, home_kernel, 1, [VM] * 5, [VM] * 4, [PROJ, *MAPS, pltpu.VMEM((3 * HD, L), F32)], [PROJ] + BUFFERS,
        pos, x, wk, wv, q, c,
    )


def away_kernel(
    pos, xs_ref, cs_ref, wk_ref, wv_ref, q_ref, st0_ref,
    x_ref, c_ref, k_ref, e_ref, g_ref, st_ref,
    v_buf, s_buf, p_buf,
):
    for n in range(0, MP, CH):
        x = xs_ref[n : n + CH].astype(BF)
        x_ref[n : n + CH] = x
        for h in range(2):
            project(h, n, x, wk_ref, wv_ref, k_ref, v_buf)
    c_ref[...] = cs_ref[...].astype(BF)

    def st(j, *rows):
        for t, row in enumerate(rows):
            st_ref[t * 8 + j : t * 8 + j + 1] = st0_ref[t * HD + j : t * HD + j + 1]
            st_ref[t * 8 + HD + j : t * 8 + HD + j + 1] = row

    attend_heads(q_ref, c_ref, e_ref, g_ref, k_ref, v_buf, s_buf, p_buf, st)


def attend_away(pos, x, c, wk, wv, q, st0):
    return call(
        AWAY, 7, away_kernel, 1, [VM] * 6, [VM] * 6,
        [pltpu.VMEM((MP, D), BF), pltpu.VMEM((L, W), BF), PROJ, *MAPS, pltpu.VMEM((24, L), F32)], [PROJ] + BUFFERS,
        pos, x, c, wk, wv, q, st0,
    )


def merge(parts):
    top = parts[0][:8]
    for p in parts[1:]:
        top = jnp.maximum(top, p[:8])
    total = delta = 0.0
    for p in parts:
        w = jnp.exp2((p[:8] - top) * EXP2)
        total += w * p[8:16]
        delta += w * p[16:24]
    return jnp.concatenate([top, total, delta], axis=0)


def place(core, mx, my, r1, r2):
    p1 = lax.rem(jnp.where(core == 1, mx, my) + r1, 4)
    p2 = lax.rem(jnp.where(core == 1, my, mx) + r2, 4)
    return jnp.where(core == 1, p1, p2), jnp.where(core == 1, p2, p1)


def weight_block(pos, r1, r2, x0_ref, x1_ref, d_ref, out):
    x, y = place(pos[0], pos[1], pos[2], r1, r2)
    rows = pl.ds(pl.multiple_of(((y % 2) * 4 + x) * 128, 128), 128)
    x0, x1 = x0_ref[:, rows].T, x1_ref[:, rows].T
    for t in range(2):
        cols = pl.ds(pl.multiple_of(t * W + y // 2 * 256, 256), 256)
        out[:, t * 256 : t * 256 + 256] = jnp.dot(x0, d_ref[:MP, cols], preferred_element_type=F32) + jnp.dot(
            x1, d_ref[MP:, cols], preferred_element_type=F32
        )


def far_kernel(
    pos, st_ref, p0_ref, p1_ref, p2_ref, p3_ref, e0_ref, g0_ref, e1_ref, g1_ref, q_ref, c0_ref, c1_ref, x0_ref, x1_ref,
    fac_ref, d_ref, away_ref, ra_ref, rb_ref,
    right, left,
):
    local = st_ref[...]
    total = merge([p0_ref[...], p1_ref[...], p2_ref[...], p3_ref[...]])
    a = jnp.exp2((local[:8] - total[:8]) * EXP2) / total[8:16]
    eps = local[16:] / local[8:16] - total[16:] / total[8:16]
    fac = jnp.concatenate([a, eps], axis=0)
    fac_ref[...] = fac
    fac = fac.T
    for n, (e_ref, g_ref, c_ref) in enumerate(((e0_ref, g0_ref, c0_ref), (e1_ref, g1_ref, c1_ref))):
        for j in range(HD):
            cols = slice(j * HS, (j + 1) * HS)
            a = fac[:, n * HD + j : n * HD + j + 1]
            eps = fac[:, 8 + n * HD + j : 8 + n * HD + j + 1]
            aq = a * q_ref[:, cols].astype(F32)
            right[j % 2, :, :HS] = (eps * aq).astype(BF)
            right[j % 2, :, HS:] = (a * c_ref[:, cols].astype(F32)).astype(BF)
            left[j % 2] = aq.astype(BF)
            for r in range(0, MP, CH):
                both = jnp.dot(e_ref[j, r : r + CH], right[j % 2], preferred_element_type=F32)
                own = jnp.dot(g_ref[j, r : r + CH], left[j % 2], preferred_element_type=F32)
                rows = slice(n * MP + r, n * MP + r + CH)
                dk, dv = ((own + both[:, :HS]) * SCALE).astype(BF), both[:, HS:].astype(BF)
                for at, part in ((j * HS, dk), (W + j * HS, dv)):
                    d_ref[rows, at : at + HS] = part
                    if n == 1:
                        away_ref[r : r + CH, at : at + HS] = part.astype(F32)
    for n, (right, left) in enumerate((((2, 0), (2, 2)), ((2, 1), (2, 3)), ((1, 2), (3, 0)), ((1, 3), (3, 1)))):
        weight_block(pos, *right, x0_ref, x1_ref, d_ref, ra_ref.at[n])
        weight_block(pos, *left, x0_ref, x1_ref, d_ref, rb_ref.at[n])


def far_grads(pos, local, parts, e0, g0, e1, g1, q, c0, c1, x0, x1):
    half = pltpu.VMEM((4, 128, 512), F32)
    return call(
        14, 8, far_kernel, 1, [VM] + [whole((24, L))] * 4 + [VM] * 9, [VM] * 5,
        [pltpu.VMEM((16, L), F32), pltpu.VMEM((2 * MP, D), BF), pltpu.VMEM((MP, D), F32), half, half],
        [pltpu.VMEM((2, L, 2 * HS), BF), pltpu.VMEM((2, L, HS), BF)],
        pos, local, *parts, e0, g0, e1, g1, q, c0, c1, x0, x1,
    )


def near_kernel(
    pos, fac_ref, e0_ref, g0_ref, k0_ref, e1_ref, g1_ref, k1_ref, x0_ref, x1_ref, d_ref,
    r0_ref, r1_ref, r3_ref, l0_ref, l1_ref, l2_ref, l3_ref,
    lat,
):

    def block(n, _):
        weight_block(pos, 0, n, x0_ref, x1_ref, d_ref, r0_ref.at[n])
        weight_block(pos, 0, n + 2, x0_ref, x1_ref, d_ref, r0_ref.at[n + 2])
        weight_block(pos, 1, n, x0_ref, x1_ref, d_ref, r1_ref.at[n])
        weight_block(pos, 3, n + 2, x0_ref, x1_ref, d_ref, r3_ref.at[n])
        return 0

    lax.fori_loop(0, 2, block, 0)
    fac = fac_ref[...].T
    for n, (e_ref, g_ref, k_ref) in enumerate(((e0_ref, g0_ref, k0_ref), (e1_ref, g1_ref, k1_ref))):
        for j in range(HD):
            a = fac[:, n * HD + j : n * HD + j + 1]
            eps = fac[:, 8 + n * HD + j : 8 + n * HD + j + 1]
            k = k_ref[j // 2, :, j % 2 * HS : j % 2 * HS + HS]
            ek = lax.dot_general(e_ref[j], k, TN, preferred_element_type=F32)
            gk = lax.dot_general(g_ref[j], k, TN, preferred_element_type=F32)
            part = (a * SCALE) * (gk + eps * ek)
            at = slice(j % 2 * HS, j % 2 * HS + HS)
            if n == 0:
                lat[j // 2, :, at] = part
            else:
                lat[j // 2, :, at] += part
    core, mx, my = pos[0], pos[1], pos[2]
    for r1, out in enumerate((l0_ref, l1_ref, l2_ref, l3_ref)):
        for r2 in range(4):
            x, y = place(core, mx, my, r1, r2)
            for z in range(8):
                row = pl.multiple_of(((y % 2) * 4 + x) * 64 + z * 8, 8)
                out[r2, z // 2 * 8 : z // 2 * 8 + 8, z % 2 * 256 : z % 2 * 256 + 256] = lat[y // 2, pl.ds(row, 8)]


def near_grads(pos, fac, e0, g0, k0, e1, g1, k1, x0, x1, d):
    block, half, lat = (pltpu.VMEM(shape, F32) for shape in ((4, 128, 512), (2, 128, 512), (4, 32, 512)))
    return call(
        14, 8, near_kernel, 1, [VM] * 10, [VM] * 7, [block, half, half] + [lat] * 4, [pltpu.VMEM((2, L, 2 * HS), F32)],
        pos, fac, e0, g0, k0, e1, g1, k1, x0, x1, d,
    )


def input_kernel(pos, d_ref, wk_ref, wv_ref, got_ref, wk_hbm, wv_hbm, out_ref, wk_buf, wv_buf, total, sems):
    theirs = pl.ds(pl.multiple_of((1 - pos[0]) * W, W), W)
    copies = [
        pltpu.make_async_copy(a.at[:, theirs], b, sems.at[n])
        for n, (a, b) in enumerate(((wk_hbm, wk_buf), (wv_hbm, wv_buf)))
    ]
    for c in copies:
        c.start()
    for r in range(0, MP, CH):
        total[r : r + CH] = lax.dot_general(
            d_ref[r : r + CH, :W], wk_ref[...], NT, preferred_element_type=F32
        ) + lax.dot_general(d_ref[r : r + CH, W:], wv_ref[...], NT, preferred_element_type=F32)
    for c in copies:
        c.wait()
    for r in range(0, MP, CH):
        got = got_ref[r : r + CH].astype(BF)
        out_ref[r : r + CH] = (
            total[r : r + CH]
            + lax.dot_general(got[:, :W], wk_buf[...], NT, preferred_element_type=F32)
            + lax.dot_general(got[:, W:], wv_buf[...], NT, preferred_element_type=F32)
        ).astype(BF)


def input_grads(pos, d, wk, wv, got, key_weight, value_weight):
    return call(
        INPUT, 5.5, input_kernel, 1, [VM] * 4 + [ANY] * 2, [whole((MP, D))], [jax.ShapeDtypeStruct((MP, D), BF)],
        [pltpu.VMEM((D, W), BF), pltpu.VMEM((D, W), BF), pltpu.VMEM((MP, D), F32), pltpu.SemaphoreType.DMA((2,))],
        pos, d, wk, wv, got, key_weight, value_weight,
    )[0]


def fold_kernel(pos, r0_ref, l0_ref, right_ref, left_ref, ra_ref, rb_ref, far_ref, *outs):
    for n, out in enumerate(outs):
        rows = slice(128 * (n % 2), 128 * (n % 2) + 128)
        if n < 2:
            out[:128] = r0_ref[n] + right_ref[rows] + rb_ref[n + 2]
        else:
            out[:128] = r0_ref[n] + left_ref[rows] + ra_ref[n]
        lat = slice(256 + 32 * n, 288 + 32 * n)
        out[128:] = l0_ref[n] + far_ref[n] + right_ref[lat] + left_ref[lat]


def fold(pos, *args):
    return call(8, 0.5, fold_kernel, 1, [VM] * 7, [VM] * 4, [pltpu.VMEM((160, 512), F32)] * 4, [], pos, *args)


def turn_kernel(pos, a_ref, b_ref, c_ref, d_ref, *outs):
    outs[4][...] = a_ref[...] + b_ref[...] + c_ref[...] + d_ref[...]
    for r in range(8):
        z = lax.rem(pos[3] + r, 8)
        out = outs[r // 2]
        out[r % 2 * 16 : r % 2 * 16 + 16] = outs[4][pl.ds(pl.multiple_of(z * 16, 16), 16)]
        rows = outs[4][pl.ds(pl.multiple_of(128 + z // 2 * 8, 8), 8)]
        out[32:40, r % 2 * 256 : r % 2 * 256 + 256] = jnp.where(z % 2 == 0, rows[:, :256], rows[:, 256:])


def turn(pos, parts):
    return call(
        8, 0.7, turn_kernel, 1, [VM] * 4, [VM] * 4, [pltpu.VMEM((40, 512), F32)] * 4,
        [pltpu.VMEM((160, 512), F32)], pos, *parts,
    )


def body(queries, inputs, cotangent, key_weight, value_weight):
    seq, batch = lax.axis_index("seq"), lax.axis_index("batch")
    yl, mx, mz = seq // 32, seq // 8 % 4, seq % 8
    yh, core = batch // 2, batch % 2
    pos = jnp.stack([core, mx, yh * 2 + yl, mz]).astype(jnp.int32)

    over = lambda y, x, z, c: (y, x, z, c + 1)
    x0, wk, wv, q, c0, xs, cs = load(pos, inputs[0], key_weight, value_weight, queries, cotangent[0])
    xs, cs = send(xs, over), send(cs, over)
    k0, e0, g0, st0 = attend_home(pos, x0, wk, wv, q, c0)
    x1, c1, k1, e1, g1, local = attend_away(pos, xs, cs, wk, wv, q, st0)

    stats = local
    stats = merge([stats] + [send(stats, lambda y, x, z, c, n=n: (y, x + n, z, c)) for n in (1, 2, 3)])
    stats = merge([stats] + [send(stats, lambda y, x, z, c, n=n: (y, x, z + n, c)) for n in (2, 4, 6)])
    parts = [stats] + [
        send(stats, lambda y, x, z, c, n=n: (y ^ (n & 1), x, z + (n >> 1), c)) for n in (1, 2, 3)
    ]

    fac, d, back, ra, rb = far_grads(pos, local, parts, e0, g0, e1, g1, q, c0, c1, x0, x1)

    def first(n):
        return lambda y, x, z, c: (y, x + n, z, c) if c == 1 else (y + n, x, z, c)

    def second(n):
        return lambda y, x, z, c: (y + n, x, z, c) if c == 1 else (y, x + n, z, c)

    ra, rb = send(ra, first(1)), send(rb, first(-1))
    r0, r1, r3, l0, l1, l2, l3 = near_grads(pos, fac, e0, g0, k0, e1, g1, k1, x0, x1, d)
    back = send(back, over)
    right = jnp.concatenate([(r1 + ra[:2]).reshape(256, 512), l1.reshape(128, 512)], axis=0)
    left = jnp.concatenate([(r3 + rb[:2]).reshape(256, 512), l3.reshape(128, 512)], axis=0)
    d, right_buf, left_buf = lax.optimization_barrier((d, right, left))
    right, left, far_l = send(right, first(1)), send(left, first(-1)), send(l2, first(2))
    grad_in = input_grads(pos, d, wk, wv, back, key_weight, value_weight)
    r0, grad_in = lax.optimization_barrier((r0, grad_in))
    parts = fold(pos, r0, l0, right, left, ra, rb, far_l)
    parts = turn(pos, [parts[0]] + [send(parts[n], second(n)) for n in (2, 1, 3)])
    parts = [parts[0]] + [send(parts[n], lambda y, x, z, c, n=n: (y, x, z + 2 * n, c)) for n in (2, 1, 3)]
    total = parts[0] + parts[1] + parts[2] + parts[3]
    here = jnp.concatenate([total[:16], jnp.concatenate([total[32:, :256], jnp.zeros((8, 256), F32)], 0)], axis=1)
    next_z = jnp.concatenate([total[16:32], jnp.concatenate([total[32:, 256:], jnp.zeros((8, 256), F32)], 0)], axis=1)
    near = here + send(next_z, lambda y, x, z, c: (y, x, z + 1, c))
    far = send(here, lambda y, x, z, c: (y + 2, x, z, c)) + send(next_z, lambda y, x, z, c: (y + 2, x, z + 1, c))
    pair = jnp.where(yh == 0, jnp.concatenate([near, far], axis=1), jnp.concatenate([far, near], axis=1))
    other = send(pair, over)
    low, high = jnp.where(core == 0, pair, other), jnp.where(core == 0, other, pair)

    def pick(start, stop, rows):
        return jnp.concatenate([a[:rows, b + start : b + stop] for a in (low, high) for b in (0, 768)], axis=1)

    return grad_in[None], pick(512, 768, 8), pick(0, 256, 16), pick(256, 512, 16)


def solution(mesh):
    placed = (P(), P("batch", "seq", None), P("batch", None, None), P(), P())
    return jax.shard_map(
        body,
        mesh=mesh,
        in_specs=placed,
        out_specs=(P("batch", "seq", None), P("seq", None), P("seq", None), P("seq", None)),
        check_vma=False,
    )
```

```python
import math

import jax
import jax.numpy as jnp
from jax import lax
from jax.experimental import pallas as pl
from jax.experimental.pallas import tpu as pltpu
from jax.sharding import PartitionSpec as P

L = 512
D = 1024
HS = 128
HD = 4
W = HD * HS
MP = 768
CH = 256
SCALE = 1.0 / math.sqrt(128.0)
EXP2 = SCALE * math.log2(math.e)
BF = jnp.bfloat16
F32 = jnp.float32
AXES = ("seq", "batch")
NT = (((1,), (1,)), ((), ()))
TN = (((0,), (0,)), ((), ()))
VM = pl.BlockSpec(memory_space=pltpu.VMEM)
ANY = pl.BlockSpec(memory_space=pl.ANY)
HOME = 12
LOADL = 52
AWAY = 12
INPUT = 24


def routes(move):
    pairs = []
    for seq in range(64):
        for batch in range(4):
            yl, x, z = seq // 32, seq // 8 % 4, seq % 8
            yh, c = batch // 2, batch % 2
            y, x, z, c = move(yh * 2 + yl, x, z, c)
            y, x, z, c = y % 4, x % 4, z % 8, c % 2
            pairs.append((seq * 4 + batch, (((y % 2) * 4 + x) * 8 + z) * 4 + (y // 2) * 2 + c))
    return pairs


def send(value, move):
    return lax.ppermute(value, AXES, routes(move))


def whole(shape):
    return pl.BlockSpec(shape, lambda i, *_: (0,) * len(shape))


def call(limit, us, kernel, grid, in_specs, out_specs, out_shape, scratch, *args):
    return pl.pallas_call(
        kernel,
        grid_spec=pltpu.PrefetchScalarGridSpec(
            num_scalar_prefetch=1, grid=(grid,), in_specs=in_specs, out_specs=out_specs, scratch_shapes=scratch
        ),
        out_shape=out_shape,
        compiler_params=pltpu.CompilerParams(vmem_limit_bytes=limit * 2**20),
        cost_estimate=pl.CostEstimate(flops=1, bytes_accessed=int(us * 3.6e6), transcendentals=0),
    )(*args)


def project(h, r, x, wk_ref, wv_ref, k_buf, v_buf):
    cols = slice(h * 256, h * 256 + 256)
    k_buf[h, r : r + CH] = jnp.dot(x, wk_ref[:, cols], preferred_element_type=F32).astype(BF)
    v_buf[h, r : r + CH] = jnp.dot(x, wv_ref[:, cols], preferred_element_type=F32).astype(BF)


def attend_heads(q_ref, c_ref, e_ref, g_ref, k_buf, v_buf, s_buf, p_buf, st):
    def multiply(j, r, top):
        h, cols, mine = j // 2, slice(j % 2 * HS, j % 2 * HS + HS), slice(j * HS, j * HS + HS)
        s = lax.dot_general(k_buf[h, r : r + CH, cols], q_ref[:, mine], NT, preferred_element_type=F32)
        s_buf[j % 2, r : r + CH] = s
        p_buf[j % 2, r : r + CH] = lax.dot_general(
            v_buf[h, r : r + CH, cols], c_ref[:, mine], NT, preferred_element_type=F32
        )
        return jnp.maximum(top, jnp.max(s.reshape(CH // 8, 8, L), axis=0))

    def weigh(j, r, top, total, delta):
        for n in range(r, r + CH, 64):
            p = jnp.exp2((s_buf[j % 2, n : n + 64] - top) * EXP2)
            s_buf[j % 2, n : n + 64] = p
            e_ref[j, n : n + 64] = p.astype(BF)
            total += jnp.sum(p.reshape(8, 8, L), axis=0)
            delta += jnp.sum((p * p_buf[j % 2, n : n + 64]).reshape(8, 8, L), axis=0)
        return total, delta

    low = jnp.full((8, L), -jnp.inf, F32)
    zero = jnp.zeros((8, L), F32)
    ahead = low
    for r in range(0, MP, CH):
        ahead = multiply(0, r, ahead)
    for j in range(HD):
        top = jnp.max(ahead, axis=0, keepdims=True)
        total, delta, ahead = zero, zero, low
        for r in range(0, MP, CH):
            if j < HD - 1:
                ahead = multiply(j + 1, r, ahead)
            total, delta = weigh(j, r, top, total, delta)
        total = jnp.sum(total, axis=0, keepdims=True)
        delta = jnp.sum(delta, axis=0, keepdims=True)
        mean = delta / total
        for n in range(0, MP, 64):
            g_ref[j, n : n + 64] = (s_buf[j % 2, n : n + 64] * (p_buf[j % 2, n : n + 64] - mean)).astype(BF)
        st(j, top, total, delta)


def load_kernel(
    pos, x_hbm, wk_hbm, wv_hbm, q_hbm, c_hbm,
    x_ref, wk_ref, wv_ref, q_ref, c_ref, xs_ref, cs_ref,
    cb, sems,
):
    mine = pl.ds(pl.multiple_of(pos[0] * W, W), W)
    theirs = pl.ds(pl.multiple_of((1 - pos[0]) * W, W), W)
    pairs = [(x_hbm.at[pl.ds(n * CH, CH)], x_ref.at[pl.ds(n * CH, CH)]) for n in range(3)]
    pairs += [(c_hbm, cb), (wk_hbm.at[:, mine], wk_ref), (wv_hbm.at[:, mine], wv_ref), (q_hbm.at[:, mine], q_ref)]
    copies = [pltpu.make_async_copy(a, b, sems.at[n]) for n, (a, b) in enumerate(pairs)]
    for c in copies:
        c.start()
    for n in range(3):
        copies[n].wait()
        xs_ref[n * CH : n * CH + CH] = x_ref[n * CH : n * CH + CH].astype(F32)
    copies[3].wait()
    c_ref[...] = cb[:, mine]
    cs_ref[...] = cb[:, theirs].astype(F32)
    for c in copies[4:]:
        c.wait()


PROJ = pltpu.VMEM((2, MP, 256), BF)
MAPS = [pltpu.VMEM((HD, MP, L), BF), pltpu.VMEM((HD, MP, L), BF)]
BUFFERS = [pltpu.VMEM((2, MP, L), F32), pltpu.VMEM((2, MP, L), F32)]


def load(pos, x, wk, wv, q, c):
    return call(
        LOADL, 4, load_kernel, 1, [ANY] * 5, [VM] * 7,
        [
            pltpu.VMEM((MP, D), BF),
            pltpu.VMEM((D, W), BF),
            pltpu.VMEM((D, W), BF),
            pltpu.VMEM((L, W), BF),
            pltpu.VMEM((L, W), BF),
            pltpu.VMEM((MP, D), F32),
            pltpu.VMEM((L, W), F32),
        ],
        [pltpu.VMEM((L, D), BF), pltpu.SemaphoreType.DMA((7,))],
        pos, x, wk, wv, q, c,
    )


def home_kernel(pos, x_ref, wk_ref, wv_ref, q_ref, c_ref, k_ref, e_ref, g_ref, st_ref, v_buf, s_buf, p_buf):
    for h in range(2):
        for r in range(0, MP, CH):
            project(h, r, x_ref[r : r + CH], wk_ref, wv_ref, k_ref, v_buf)

    def st(j, *rows):
        for t, row in enumerate(rows):
            st_ref[t * HD + j : t * HD + j + 1] = row

    attend_heads(q_ref, c_ref, e_ref, g_ref, k_ref, v_buf, s_buf, p_buf, st)


def attend_home(pos, x, wk, wv, q, c):
    return call(
        HOME, 7, home_kernel, 1, [VM] * 5, [VM] * 4, [PROJ, *MAPS, pltpu.VMEM((3 * HD, L), F32)], [PROJ] + BUFFERS,
        pos, x, wk, wv, q, c,
    )


def away_kernel(
    pos, xs_ref, cs_ref, wk_ref, wv_ref, q_ref, st0_ref,
    x_ref, c_ref, k_ref, e_ref, g_ref, st_ref,
    v_buf, s_buf, p_buf,
):
    for n in range(0, MP, CH):
        x = xs_ref[n : n + CH].astype(BF)
        x_ref[n : n + CH] = x
        for h in range(2):
            project(h, n, x, wk_ref, wv_ref, k_ref, v_buf)
    c_ref[...] = cs_ref[...].astype(BF)

    def st(j, *rows):
        for t, row in enumerate(rows):
            st_ref[t * 8 + j : t * 8 + j + 1] = st0_ref[t * HD + j : t * HD + j + 1]
            st_ref[t * 8 + HD + j : t * 8 + HD + j + 1] = row

    attend_heads(q_ref, c_ref, e_ref, g_ref, k_ref, v_buf, s_buf, p_buf, st)


def attend_away(pos, x, c, wk, wv, q, st0):
    return call(
        AWAY, 7, away_kernel, 1, [VM] * 6, [VM] * 6,
        [pltpu.VMEM((MP, D), BF), pltpu.VMEM((L, W), BF), PROJ, *MAPS, pltpu.VMEM((24, L), F32)], [PROJ] + BUFFERS,
        pos, x, c, wk, wv, q, st0,
    )


def merge(parts):
    top = parts[0][:8]
    for p in parts[1:]:
        top = jnp.maximum(top, p[:8])
    total = delta = 0.0
    for p in parts:
        w = jnp.exp2((p[:8] - top) * EXP2)
        total += w * p[8:16]
        delta += w * p[16:24]
    return jnp.concatenate([top, total, delta], axis=0)


def place(core, mx, my, r1, r2):
    p1 = lax.rem(jnp.where(core == 1, mx, my) + r1, 4)
    p2 = lax.rem(jnp.where(core == 1, my, mx) + r2, 4)
    return jnp.where(core == 1, p1, p2), jnp.where(core == 1, p2, p1)


def weight_block(pos, r1, r2, x0_ref, x1_ref, d_ref, out):
    x, y = place(pos[0], pos[1], pos[2], r1, r2)
    rows = pl.ds(pl.multiple_of(((y % 2) * 4 + x) * 128, 128), 128)
    x0, x1 = x0_ref[:, rows].T, x1_ref[:, rows].T
    for t in range(2):
        cols = pl.ds(pl.multiple_of(t * W + y // 2 * 256, 256), 256)
        out[:, t * 256 : t * 256 + 256] = jnp.dot(x0, d_ref[:MP, cols], preferred_element_type=F32) + jnp.dot(
            x1, d_ref[MP:, cols], preferred_element_type=F32
        )


def far_kernel(
    pos, st_ref, p0_ref, p1_ref, p2_ref, p3_ref, e0_ref, g0_ref, e1_ref, g1_ref, q_ref, c0_ref, c1_ref, x0_ref, x1_ref,
    fac_ref, d_ref, away_ref, ra_ref, rb_ref,
    right, left,
):
    local = st_ref[...]
    total = merge([p0_ref[...], p1_ref[...], p2_ref[...], p3_ref[...]])
    a = jnp.exp2((local[:8] - total[:8]) * EXP2) / total[8:16]
    eps = local[16:] / local[8:16] - total[16:] / total[8:16]
    fac = jnp.concatenate([a, eps], axis=0)
    fac_ref[...] = fac
    fac = fac.T
    for n, (e_ref, g_ref, c_ref) in enumerate(((e0_ref, g0_ref, c0_ref), (e1_ref, g1_ref, c1_ref))):
        for j in range(HD):
            cols = slice(j * HS, (j + 1) * HS)
            a = fac[:, n * HD + j : n * HD + j + 1]
            eps = fac[:, 8 + n * HD + j : 8 + n * HD + j + 1]
            aq = a * q_ref[:, cols].astype(F32)
            right[j % 2, :, :HS] = (eps * aq).astype(BF)
            right[j % 2, :, HS:] = (a * c_ref[:, cols].astype(F32)).astype(BF)
            left[j % 2] = aq.astype(BF)
            for r in range(0, MP, CH):
                both = jnp.dot(e_ref[j, r : r + CH], right[j % 2], preferred_element_type=F32)
                own = jnp.dot(g_ref[j, r : r + CH], left[j % 2], preferred_element_type=F32)
                rows = slice(n * MP + r, n * MP + r + CH)
                dk, dv = ((own + both[:, :HS]) * SCALE).astype(BF), both[:, HS:].astype(BF)
                for at, part in ((j * HS, dk), (W + j * HS, dv)):
                    d_ref[rows, at : at + HS] = part
                    if n == 1:
                        away_ref[r : r + CH, at : at + HS] = part.astype(F32)
    for n, (right, left) in enumerate((((2, 0), (2, 2)), ((2, 1), (2, 3)), ((1, 2), (3, 0)), ((1, 3), (3, 1)))):
        weight_block(pos, *right, x0_ref, x1_ref, d_ref, ra_ref.at[n])
        weight_block(pos, *left, x0_ref, x1_ref, d_ref, rb_ref.at[n])


def far_grads(pos, local, parts, e0, g0, e1, g1, q, c0, c1, x0, x1):
    half = pltpu.VMEM((4, 128, 512), F32)
    return call(
        14, 8, far_kernel, 1, [VM] + [whole((24, L))] * 4 + [VM] * 9, [VM] * 5,
        [pltpu.VMEM((16, L), F32), pltpu.VMEM((2 * MP, D), BF), pltpu.VMEM((MP, D), F32), half, half],
        [pltpu.VMEM((2, L, 2 * HS), BF), pltpu.VMEM((2, L, HS), BF)],
        pos, local, *parts, e0, g0, e1, g1, q, c0, c1, x0, x1,
    )


def near_kernel(
    pos, fac_ref, e0_ref, g0_ref, k0_ref, e1_ref, g1_ref, k1_ref, x0_ref, x1_ref, d_ref,
    r0_ref, r1_ref, r3_ref, l0_ref, l1_ref, l2_ref, l3_ref,
    lat,
):

    def block(n, _):
        weight_block(pos, 0, n, x0_ref, x1_ref, d_ref, r0_ref.at[n])
        weight_block(pos, 0, n + 2, x0_ref, x1_ref, d_ref, r0_ref.at[n + 2])
        weight_block(pos, 1, n, x0_ref, x1_ref, d_ref, r1_ref.at[n])
        weight_block(pos, 3, n + 2, x0_ref, x1_ref, d_ref, r3_ref.at[n])
        return 0

    lax.fori_loop(0, 2, block, 0)
    fac = fac_ref[...].T
    for n, (e_ref, g_ref, k_ref) in enumerate(((e0_ref, g0_ref, k0_ref), (e1_ref, g1_ref, k1_ref))):
        for j in range(HD):
            a = fac[:, n * HD + j : n * HD + j + 1]
            eps = fac[:, 8 + n * HD + j : 8 + n * HD + j + 1]
            k = k_ref[j // 2, :, j % 2 * HS : j % 2 * HS + HS]
            ek = lax.dot_general(e_ref[j], k, TN, preferred_element_type=F32)
            gk = lax.dot_general(g_ref[j], k, TN, preferred_element_type=F32)
            part = (a * SCALE) * (gk + eps * ek)
            at = slice(j % 2 * HS, j % 2 * HS + HS)
            if n == 0:
                lat[j // 2, :, at] = part
            else:
                lat[j // 2, :, at] += part
    core, mx, my = pos[0], pos[1], pos[2]
    for r1, out in enumerate((l0_ref, l1_ref, l2_ref, l3_ref)):
        for r2 in range(4):
            x, y = place(core, mx, my, r1, r2)
            for z in range(8):
                row = pl.multiple_of(((y % 2) * 4 + x) * 64 + z * 8, 8)
                out[r2, z // 2 * 8 : z // 2 * 8 + 8, z % 2 * 256 : z % 2 * 256 + 256] = lat[y // 2, pl.ds(row, 8)]


def near_grads(pos, fac, e0, g0, k0, e1, g1, k1, x0, x1, d):
    block, half, lat = (pltpu.VMEM(shape, F32) for shape in ((4, 128, 512), (2, 128, 512), (4, 32, 512)))
    return call(
        14, 8, near_kernel, 1, [VM] * 10, [VM] * 7, [block, half, half] + [lat] * 4, [pltpu.VMEM((2, L, 2 * HS), F32)],
        pos, fac, e0, g0, k0, e1, g1, k1, x0, x1, d,
    )


def input_kernel(pos, d_ref, wk_ref, wv_ref, got_ref, wk_hbm, wv_hbm, out_ref, wk_buf, wv_buf, total, sems):
    theirs = pl.ds(pl.multiple_of((1 - pos[0]) * W, W), W)
    copies = [
        pltpu.make_async_copy(a.at[:, theirs], b, sems.at[n])
        for n, (a, b) in enumerate(((wk_hbm, wk_buf), (wv_hbm, wv_buf)))
    ]
    for c in copies:
        c.start()
    for r in range(0, MP, CH):
        total[r : r + CH] = lax.dot_general(
            d_ref[r : r + CH, :W], wk_ref[...], NT, preferred_element_type=F32
        ) + lax.dot_general(d_ref[r : r + CH, W:], wv_ref[...], NT, preferred_element_type=F32)
    for c in copies:
        c.wait()
    for r in range(0, MP, CH):
        got = got_ref[r : r + CH].astype(BF)
        out_ref[r : r + CH] = (
            total[r : r + CH]
            + lax.dot_general(got[:, :W], wk_buf[...], NT, preferred_element_type=F32)
            + lax.dot_general(got[:, W:], wv_buf[...], NT, preferred_element_type=F32)
        ).astype(BF)


def input_grads(pos, d, wk, wv, got, key_weight, value_weight):
    return call(
        INPUT, 5.5, input_kernel, 1, [VM] * 4 + [ANY] * 2, [whole((MP, D))], [jax.ShapeDtypeStruct((MP, D), BF)],
        [pltpu.VMEM((D, W), BF), pltpu.VMEM((D, W), BF), pltpu.VMEM((MP, D), F32), pltpu.SemaphoreType.DMA((2,))],
        pos, d, wk, wv, got, key_weight, value_weight,
    )[0]


def fold_kernel(pos, r0_ref, l0_ref, right_ref, left_ref, ra_ref, rb_ref, far_ref, *outs):
    for n, out in enumerate(outs):
        rows = slice(128 * (n % 2), 128 * (n % 2) + 128)
        if n < 2:
            out[:128] = r0_ref[n] + right_ref[rows] + rb_ref[n + 2]
        else:
            out[:128] = r0_ref[n] + left_ref[rows] + ra_ref[n]
        lat = slice(256 + 32 * n, 288 + 32 * n)
        out[128:] = l0_ref[n] + far_ref[n] + right_ref[lat] + left_ref[lat]


def fold(pos, *args):
    return call(8, 0.5, fold_kernel, 1, [VM] * 7, [VM] * 4, [pltpu.VMEM((160, 512), F32)] * 4, [], pos, *args)


def turn_kernel(pos, a_ref, b_ref, c_ref, d_ref, *outs):
    outs[4][...] = a_ref[...] + b_ref[...] + c_ref[...] + d_ref[...]
    for r in range(8):
        z = lax.rem(pos[3] + r, 8)
        out = outs[r // 2]
        out[r % 2 * 16 : r % 2 * 16 + 16] = outs[4][pl.ds(pl.multiple_of(z * 16, 16), 16)]
        rows = outs[4][pl.ds(pl.multiple_of(128 + z // 2 * 8, 8), 8)]
        out[32:40, r % 2 * 256 : r % 2 * 256 + 256] = jnp.where(z % 2 == 0, rows[:, :256], rows[:, 256:])


def turn(pos, parts):
    return call(
        8, 0.7, turn_kernel, 1, [VM] * 4, [VM] * 4, [pltpu.VMEM((40, 512), F32)] * 4,
        [pltpu.VMEM((160, 512), F32)], pos, *parts,
    )


def finish_kernel(pos, mine_ref, other_ref, latent_ref, key_ref, value_ref):
    for c in range(2):
        src = jnp.where(pos[0] == c, mine_ref[...], other_ref[...])
        for y in range(2):
            to, at = slice(c * W + y * 256, c * W + y * 256 + 256), y * 768
            key_ref[:, to] = src[:, at : at + 256]
            value_ref[:, to] = src[:, at + 256 : at + 512]
            latent_ref[:, to] = src[:8, at + 512 : at + 768]


def body(queries, inputs, cotangent, key_weight, value_weight):
    seq, batch = lax.axis_index("seq"), lax.axis_index("batch")
    yl, mx, mz = seq // 32, seq // 8 % 4, seq % 8
    yh, core = batch // 2, batch % 2
    pos = jnp.stack([core, mx, yh * 2 + yl, mz]).astype(jnp.int32)

    over = lambda y, x, z, c: (y, x, z, c + 1)
    x0, wk, wv, q, c0, xs, cs = load(pos, inputs[0], key_weight, value_weight, queries, cotangent[0])
    xs, cs = send(xs, over), send(cs, over)
    k0, e0, g0, st0 = attend_home(pos, x0, wk, wv, q, c0)
    x1, c1, k1, e1, g1, local = attend_away(pos, xs, cs, wk, wv, q, st0)

    stats = local
    stats = merge([stats] + [send(stats, lambda y, x, z, c, n=n: (y, x + n, z, c)) for n in (1, 2, 3)])
    stats = merge([stats] + [send(stats, lambda y, x, z, c, n=n: (y, x, z + n, c)) for n in (2, 4, 6)])
    parts = [stats] + [
        send(stats, lambda y, x, z, c, n=n: (y ^ (n & 1), x, z + (n >> 1), c)) for n in (1, 2, 3)
    ]

    fac, d, back, ra, rb = far_grads(pos, local, parts, e0, g0, e1, g1, q, c0, c1, x0, x1)

    def first(n):
        return lambda y, x, z, c: (y, x + n, z, c) if c == 1 else (y + n, x, z, c)

    def second(n):
        return lambda y, x, z, c: (y + n, x, z, c) if c == 1 else (y, x + n, z, c)

    ra, rb = send(ra, first(1)), send(rb, first(-1))
    r0, r1, r3, l0, l1, l2, l3 = near_grads(pos, fac, e0, g0, k0, e1, g1, k1, x0, x1, d)
    back = send(back, over)
    right = jnp.concatenate([(r1 + ra[:2]).reshape(256, 512), l1.reshape(128, 512)], axis=0)
    left = jnp.concatenate([(r3 + rb[:2]).reshape(256, 512), l3.reshape(128, 512)], axis=0)
    d, right_buf, left_buf = lax.optimization_barrier((d, right, left))
    right, left, far_l = send(right, first(1)), send(left, first(-1)), send(l2, first(2))
    grad_in = input_grads(pos, d, wk, wv, back, key_weight, value_weight)
    r0, grad_in = lax.optimization_barrier((r0, grad_in))
    parts = fold(pos, r0, l0, right, left, ra, rb, far_l)
    parts = turn(pos, [parts[0]] + [send(parts[n], second(n)) for n in (2, 1, 3)])
    parts = [parts[0]] + [send(parts[n], lambda y, x, z, c, n=n: (y, x, z + 2 * n, c)) for n in (2, 1, 3)]
    total = parts[0] + parts[1] + parts[2] + parts[3]
    here = jnp.concatenate([total[:16], jnp.concatenate([total[32:, :256], jnp.zeros((8, 256), F32)], 0)], axis=1)
    next_z = jnp.concatenate([total[16:32], jnp.concatenate([total[32:, 256:], jnp.zeros((8, 256), F32)], 0)], axis=1)
    near = here + send(next_z, lambda y, x, z, c: (y, x, z + 1, c))
    far = send(here, lambda y, x, z, c: (y + 2, x, z, c)) + send(next_z, lambda y, x, z, c: (y + 2, x, z + 1, c))
    pair = jnp.where(yh == 0, jnp.concatenate([near, far], axis=1), jnp.concatenate([far, near], axis=1))
    other = send(pair, over)
    latent_grad, key_grad, value_grad = call(
        8, 0.7, finish_kernel, 1, [VM] * 2, [whole((8, D)), whole((16, D)), whole((16, D))],
        [jax.ShapeDtypeStruct((8, D), F32)] + [jax.ShapeDtypeStruct((16, D), F32)] * 2, [], pos, pair, other,
    )
    return grad_in[None], latent_grad, key_grad, value_grad


def solution(mesh):
    placed = (P(), P("batch", "seq", None), P("batch", None, None), P(), P())
    return jax.shard_map(
        body,
        mesh=mesh,
        in_specs=placed,
        out_specs=(P("batch", "seq", None), P("seq", None), P("seq", None), P("seq", None)),
        check_vma=False,
    )
```
